32 devices in a mesh: seq: 8 (over y, x, core), fsdp: 4 (over z).
Axes of the slice: x: 2, y: 2, z: 4, core: 2. Of those that a mesh axis runs over, the one named last changes fastest.
Arguments:
- tokens: bfloat16 [4, 1536, 2048], P('fsdp', 'seq'), may hold values from -41 to 41
- cotangent: bfloat16 [4, 1536, 2048], P('fsdp', 'seq'), may hold values from -6 to 6
- attn_gain: bfloat16 [2048], P(('seq', 'fsdp')), may hold values from 0.099609375 to 1.8984375
- mlp_gain: bfloat16 [2048], P(('seq', 'fsdp')), may hold values from 0.099609375 to 1.8984375
- w_q: bfloat16 [2048, 2048], P(('seq', 'fsdp')), may hold values from -0.1875 to 0.1875
- w_k: bfloat16 [2048, 2048], P(('seq', 'fsdp')), may hold values from -0.1875 to 0.1875
- w_v: bfloat16 [2048, 2048], P(('seq', 'fsdp')), may hold values from -0.125 to 0.125
- w_o: bfloat16 [2048, 2048], P(('seq', 'fsdp')), may hold values from -0.5 to 0.5
- w_gate: bfloat16 [2048, 8192], P(('seq', 'fsdp')), may hold values from -0.125 to 0.125
- w_up: bfloat16 [2048, 8192], P(('seq', 'fsdp')), may hold values from -0.125 to 0.125
- w_down: bfloat16 [8192, 2048], P(('seq', 'fsdp')), may hold values from -0.0625 to 0.0625
Outputs:
- layer_out: bfloat16 [4, 1536, 2048], P('fsdp', 'seq')
- input_grad: bfloat16 [4, 1536, 2048], P('fsdp', 'seq')
- attn_gain_grad: float32 [2048], P(('seq', 'fsdp'))
- mlp_gain_grad: float32 [2048], P(('seq', 'fsdp'))
- w_q_grad: float32 [2048, 2048], P(('seq', 'fsdp'))
- w_k_grad: float32 [2048, 2048], P(('seq', 'fsdp'))
- w_v_grad: float32 [2048, 2048], P(('seq', 'fsdp'))
- w_o_grad: float32 [2048, 2048], P(('seq', 'fsdp'))
- w_gate_grad: float32 [2048, 8192], P(('seq', 'fsdp'))
- w_up_grad: float32 [2048, 8192], P(('seq', 'fsdp'))
- w_down_grad: float32 [8192, 2048], P(('seq', 'fsdp'))
The draws below stay inside these ranges and needn't reach their ends.
All inputs are finite; a program needn't handle non-finite values.
Results may differ from the reference program's by a relative error of at most 0.017.
Values may be sent and summed in bfloat16 or wider, within the bound.
No kernel may reach another device: no remote copies, remote signals or barrier semaphores. Data moves between devices by JAX's collectives and lax.ppermute only.
A program may use at most 576 MiB of HBM per device.

```python
import math
import jax
import jax.numpy as jnp
from jax import lax

D = 2048
HEADS = 32
HD = 64
FF = 8192
SEQ_LEN = 1536
SEQS = 4


def draw_tokens(key, part):
    key = jax.random.fold_in(key, 17)
    key_base, key_column, key_row = jax.random.split(key, 3)
    base = jnp.clip(jax.random.normal(key_base, (SEQS, SEQ_LEN, D), jnp.float32), -6.0, 6.0)
    spread = 10.0
    column_scale = jnp.exp(jax.random.uniform(key_column, (D,), jnp.float32, 0.0, math.log(10.0))) / 4.64
    row_scale = jnp.exp(jax.random.uniform(key_row, (SEQS, SEQ_LEN, 1), jnp.float32, 0.0, math.log(spread))) / math.sqrt(spread)
    return (base * column_scale * row_scale).astype(jnp.bfloat16)


def block_scale(key, shape, shards, low, top_value):
    def one(dim, shards_of):
        draws = jax.random.uniform(jax.random.fold_in(jax.random.fold_in(key, 6), dim), (shards_of,), jnp.float32, low / len(shards), top_value / len(shards))
        return jnp.repeat(jnp.exp(draws), shape[dim] // shards_of).reshape((-1,) + (1,) * (len(shape) - dim - 1))

    loudness = one(*shards[0])
    for cut in shards[1:]:
        loudness = loudness * one(*cut)
    return loudness


def gaussian(rng, shape, scale, bound, cuts=(), held_as=jnp.bfloat16):
    entries = scale * jax.random.normal(rng, shape, jnp.float32)
    if cuts:
        entries = entries * block_scale(rng, shape, cuts, -0.22, 0.18)
    return jnp.clip(entries, -bound, bound).astype(held_as)


def setup_inputs(seed: int = 0) -> dict:
    splits = jax.random.split(jax.random.key(seed), 12)
    return {
        "tokens": draw_tokens(jax.random.fold_in(splits[11], 71), 0),
        "cotangent": gaussian(splits[1], (SEQS, SEQ_LEN, D), 1.0, 6.0, ((0, 4), (1, 8))),
        "attn_gain": jnp.clip(1.0 + 0.18 * jax.random.normal(splits[2], (D,), jnp.float32), 0.099609375, 1.8984375).astype(jnp.bfloat16),
        "mlp_gain": jnp.clip(1.0 + 0.18 * jax.random.normal(splits[3], (D,), jnp.float32), 0.099609375, 1.8984375).astype(jnp.bfloat16),
        "w_q": gaussian(splits[4], (D, D), (D // 2) ** -0.5, 0.1875, ((0, 32),)),
        "w_k": gaussian(splits[5], (D, D), (D // 2) ** -0.5, 0.1875, ((0, 32),)),
        "w_v": gaussian(splits[6], (D, D), D ** -0.5, 0.125, ((0, 32),)),
        "w_o": gaussian(splits[7], (D, D), (D // 16) ** -0.5, 0.5, ((0, 32),)),
        "w_gate": gaussian(splits[8], (D, FF), D ** -0.5, 0.125, ((0, 32),)),
        "w_up": gaussian(splits[9], (D, FF), D ** -0.5, 0.125, ((0, 32),)),
        "w_down": gaussian(splits[10], (FF, D), FF ** -0.5, 0.0625, ((0, 32),)),
    }


EPS = 1e-05
THETA = 130000.0

@jax.custom_vjp
def low(v):
    return lax.optimization_barrier(v.astype(jnp.bfloat16)).astype(jnp.float32)

@jax.custom_vjp
def low_back(v):
    return v

def low_keep(v):
    return (low(v), None)

def low_pass(kept, grad):
    return (grad,)

def back_keep(v):
    return (v, None)

def back_low(kept, grad):
    return (low(grad),)
low.defvjp(low_keep, low_pass)
low_back.defvjp(back_keep, back_low)

def matmul(left, right):
    return jnp.dot(left, right, precision=lax.Precision.HIGHEST, preferred_element_type=jnp.float32)

def rms_scale(values):
    return lax.rsqrt(lax.optimization_barrier(jnp.mean(values * values, axis=-1, keepdims=True)) + EPS)

def rotary_tables(positions):
    halfway = HD // 2
    frequency = THETA ** (-(jnp.arange(halfway, dtype=jnp.float32) * 2.0) / HD)
    angles = positions.astype(jnp.float32)[:, None] * frequency[None, :]
    cosine = jnp.cos(angles)
    sine = jnp.sin(angles)
    return (jnp.concatenate([cosine, cosine], -1)[:, None, :], jnp.concatenate([sine, sine], -1)[:, None, :])

def rotate(values):
    halfway = values.shape[-1] // 2
    return jnp.concatenate([-values[..., halfway:], values[..., :halfway]], -1)

def rotary(values, cosine, sine):
    return values * cosine + rotate(values) * sine

def attend(queries, keys_all, values):
    block = min(512, SEQ_LEN)
    scale = HD ** (-0.5)
    key_places = jnp.arange(SEQ_LEN, dtype=jnp.int32)

    def one_block(start):
        query_block = lax.dynamic_slice_in_dim(queries, start, block, 0)
        scores = low_back(jnp.einsum('qhd,khd->hqk', query_block, keys_all, precision=lax.Precision.HIGHEST) * scale)
        places = start + jnp.arange(block, dtype=jnp.int32)
        allowed = key_places[None, :] <= places[:, None]
        scores = jnp.where(allowed[None], scores, -1e+30)
        highest = lax.optimization_barrier(jnp.max(scores, axis=-1, keepdims=True))
        weights = jnp.exp(scores - highest)
        probs = low(weights / lax.optimization_barrier(jnp.sum(weights, axis=-1, keepdims=True)))
        return jnp.einsum('hqk,khd->qhd', probs, values, precision=lax.Precision.HIGHEST)
    starts = jnp.arange(SEQ_LEN // block, dtype=jnp.int32) * block
    blocks = lax.map(jax.checkpoint(one_block), starts)
    return blocks.reshape(SEQ_LEN, HEADS * HD)

def layer(rows_in, attn_gain, mlp_gain, w_q, w_k, w_v, w_o, w_gate, w_up, w_down):
    cosine, sine = rotary_tables(jnp.arange(SEQ_LEN, dtype=jnp.int32))
    normed = low(rows_in * rms_scale(rows_in) * attn_gain)
    queries = low_back(matmul(normed, w_q)).reshape(SEQ_LEN, HEADS, HD)
    queries = low_back(low(rotary(queries, cosine, sine)))
    keys_all = low_back(matmul(normed, w_k)).reshape(SEQ_LEN, HEADS, HD)
    keys_all = low_back(low(rotary(keys_all, cosine, sine)))
    values = low_back(low(matmul(normed, w_v))).reshape(SEQ_LEN, HEADS, HD)
    attended = low_back(low(attend(queries, keys_all, values)))
    middle = rows_in + low_back(matmul(attended, w_o))
    normed_mlp = low(middle * rms_scale(middle) * mlp_gain)
    gate_pre = low_back(matmul(normed_mlp, w_gate))
    up_pre = low_back(matmul(normed_mlp, w_up))
    mixed = low(jax.nn.silu(gate_pre) * up_pre)
    return middle + matmul(mixed, w_down)

def reference(tokens, cotangent, attn_gain, mlp_gain, w_q, w_k, w_v, w_o, w_gate, w_up, w_down):
    params = tuple((weight.astype(jnp.float32) for weight in (attn_gain, mlp_gain, w_q, w_k, w_v, w_o, w_gate, w_up, w_down)))

    def step(totals, pair):
        rows_in, grad_out = pair
        result, pullback = jax.vjp(layer, rows_in, *params)
        grads = pullback(grad_out)
        totals = tuple((total + grad for total, grad in zip(totals, grads[1:])))
        return (totals, (result.astype(jnp.bfloat16), grads[0].astype(jnp.bfloat16)))
    zeros = tuple((jnp.zeros_like(weight) for weight in params))
    totals, (layer_out, input_grad) = lax.scan(step, zeros, (tokens.astype(jnp.float32), cotangent.astype(jnp.float32)))
    return (layer_out, input_grad, totals[0], totals[1], totals[2], totals[3], totals[4], totals[5], totals[6], totals[7], totals[8])
```

```python
import functools

import jax
import jax.numpy as jnp
from jax import lax
from jax.sharding import PartitionSpec as P

HEADS = 32
HD = 64


EPS = 1e-05
THETA = 130000.0

F32 = jnp.float32
LOW = jnp.bfloat16


def rms_scale(values):
    return lax.rsqrt(jnp.mean(values * values, axis=-1, keepdims=True) + EPS)


def rotary_tables(positions):
    halfway = HD // 2
    frequency = THETA ** (-(jnp.arange(halfway, dtype=F32) * 2.0) / HD)
    angles = positions.astype(F32)[:, None] * frequency[None, :]
    cosine = jnp.cos(angles)
    sine = jnp.sin(angles)
    return (
        jnp.concatenate([cosine, cosine], -1)[:, None, :],
        jnp.concatenate([sine, sine], -1)[:, None, :],
    )


def rotate(values):
    halfway = values.shape[-1] // 2
    return jnp.concatenate([-values[..., halfway:], values[..., :halfway]], -1)


def rotary(values, cosine, sine):
    return values * cosine + rotate(values) * sine


def rotary_back(values, cosine, sine):
    return values * cosine - rotate(values * sine)


def masked_scores(query_block, key_heads, query_places, key_places):
    scores = jnp.einsum(
        "qhd,khd->hqk", query_block, key_heads, preferred_element_type=F32
    ) * HD ** (-0.5)
    allowed = key_places[None, :] <= query_places[:, None]
    return jnp.where(allowed[None], scores, -1e30)


def attend_forward(queries, keys_all, values, places):
    length = queries.shape[0]
    heads = queries.shape[1] // HD
    block = min(512, length)
    count = length // block
    query_blocks = queries.reshape(count, block, heads, HD)
    key_heads = keys_all.reshape(length, heads, HD)
    value_heads = values.reshape(length, heads, HD)

    def one_block(pair):
        query_block, query_places = pair
        scores = masked_scores(query_block, key_heads, query_places, places)
        highest = jnp.max(scores, axis=-1, keepdims=True)
        weights = jnp.exp(scores - highest)
        totals = jnp.sum(weights, axis=-1, keepdims=True)
        probs = (weights / totals).astype(LOW)
        output = jnp.einsum("hqk,khd->qhd", probs, value_heads, preferred_element_type=F32)
        return (output.astype(LOW), (highest + jnp.log(totals))[..., 0])

    outputs, log_totals = lax.map(one_block, (query_blocks, places.reshape(count, block)))
    return (outputs.reshape(length, heads * HD), log_totals)


def attend_backward(queries, keys_all, values, grad_heads, log_totals, places):
    length = queries.shape[0]
    heads = queries.shape[1] // HD
    block = min(512, length)
    count = length // block
    scale = HD ** (-0.5)
    query_blocks = queries.reshape(count, block, heads, HD)
    grad_blocks = grad_heads.reshape(count, block, heads, HD)
    key_heads = keys_all.reshape(length, heads, HD)
    value_heads = values.reshape(length, heads, HD)

    def one_block(carry, inputs):
        key_sum, value_sum = carry
        query_block, grad_block, log_block, query_places = inputs
        scores = masked_scores(query_block, key_heads, query_places, places)
        probs = jnp.exp(scores - log_block[..., None])
        grad_probs = jnp.einsum(
            "qhd,khd->hqk", grad_block, value_heads, preferred_element_type=F32
        )
        inner = jnp.sum(probs * grad_probs, axis=-1, keepdims=True)
        grad_scores = (probs * (grad_probs - inner)).astype(LOW)
        grad_query = (
            jnp.einsum("hqk,khd->qhd", grad_scores, key_heads, preferred_element_type=F32) * scale
        )
        key_sum = (
            key_sum
            + jnp.einsum("hqk,qhd->khd", grad_scores, query_block, preferred_element_type=F32)
            * scale
        )
        value_sum = value_sum + jnp.einsum(
            "hqk,qhd->khd", probs.astype(LOW), grad_block, preferred_element_type=F32
        )
        return ((key_sum, value_sum), grad_query.astype(LOW))

    empty = jnp.zeros((length, heads, HD), F32)
    (key_sum, value_sum), grad_queries = lax.scan(
        one_block, (empty, empty), (query_blocks, grad_blocks, log_totals, places.reshape(count, block))
    )
    return (
        grad_queries.reshape(length, heads * HD),
        key_sum.astype(LOW).reshape(length, heads * HD),
        value_sum.astype(LOW).reshape(length, heads * HD),
    )


def flip(values, axis, count, mask):
    return lax.ppermute(values, axis, [(i, i ^ mask) for i in range(count)])


def bits_of(count):
    return list(range(count.bit_length() - 1))


def token_bits(count, half):
    bits = bits_of(count)
    return bits[:1] + (bits[1:] if half == 0 else bits[:0:-1])


def token_places(count, rows):
    me = lax.axis_index("seq")
    places = []
    for half in (0, 1):
        ranks = [0]
        for bit in reversed(token_bits(count, half)):
            ranks = ranks + [rank ^ (1 << bit) for rank in ranks]
        for rank in ranks:
            places.append((me ^ rank) * rows + half * (rows // 2) + jnp.arange(rows // 2, dtype=jnp.int32))
    return jnp.concatenate(places)


def gather_tokens(values, count):
    rows = values.shape[0] // 2
    halves = []
    for half in (0, 1):
        blocks = [values[half * rows : (half + 1) * rows]]
        for bit in reversed(token_bits(count, half)):
            blocks = blocks + [flip(block, "seq", count, 1 << bit) for block in blocks]
        halves.append(jnp.concatenate(blocks, 0))
    return halves


def reduce_tokens(part, size, count):
    outs = []
    for half in (0, 1):
        bits = token_bits(count, half)
        got = flip(part(half, size // 2, size).astype(LOW), "seq", count, 1 << bits[0])
        kept = part(half, 0, size // 2) + got.astype(F32)
        for bit in bits[1:]:
            middle = kept.shape[0] // 2
            got = flip(kept[middle:].astype(LOW), "seq", count, 1 << bit)
            kept = kept[:middle] + got.astype(F32)
        outs.append(kept)
    return jnp.concatenate(outs, 0)


def gather_rows(piece, count):
    me = lax.axis_index("fsdp")
    pieces = [(0, piece)]
    for bit in reversed(bits_of(count)):
        pieces = pieces + [(j ^ (1 << bit), flip(p, "fsdp", count, 1 << bit)) for j, p in pieces]
    outer, rows, width = piece.shape
    whole = jnp.zeros((outer, count, rows, width), piece.dtype)
    for j, p in pieces:
        whole = lax.dynamic_update_slice(whole, p[:, None], (0, me ^ j, 0, 0))
    return whole


def reduce_rows(whole, count):
    me = lax.axis_index("fsdp")
    outer, _, rows, width = whole.shape
    left = count
    for bit in bits_of(count):
        mine = (me >> bit) & 1
        pairs = whole.reshape(outer, left // 2, 2, rows, width)
        sent = lax.dynamic_slice_in_dim(pairs, 1 - mine, 1, 2).astype(LOW)
        kept = lax.dynamic_slice_in_dim(pairs, mine, 1, 2)
        got = flip(sent, "fsdp", count, 1 << bit)
        whole = kept.astype(F32) + got.astype(F32)
        left //= 2
    return whole.reshape(outer, rows, width)


def gather_small(values, counts):
    for axis in ("fsdp", "seq"):
        count = counts[axis]
        me = lax.axis_index(axis)
        for bit in bits_of(count):
            other = flip(values, axis, count, 1 << bit)
            mine = (me >> bit) & 1
            values = jnp.where(
                mine == 0,
                jnp.concatenate([values, other], -1),
                jnp.concatenate([other, values], -1),
            )
    return values


def scatter_small(values, counts):
    for axis in ("seq", "fsdp"):
        count = counts[axis]
        me = lax.axis_index(axis)
        for bit in reversed(bits_of(count)):
            mine = (me >> bit) & 1
            middle = values.shape[-1] // 2
            low, high = values[..., :middle], values[..., middle:]
            sent = jnp.where(mine == 0, high, low)
            values = jnp.where(mine == 0, low, high) + flip(sent, axis, count, 1 << bit)
    return values


def per_device(
    counts, tokens, cotangent, attn_gain, mlp_gain, w_q, w_k, w_v, w_o, w_gate, w_up, w_down
):
    seq, fsdp = counts["seq"], counts["fsdp"]
    rows = tokens.shape[1]
    width = tokens.shape[2]
    size = rows // 2 * seq
    inputs = tokens[0].astype(F32)
    own_grad = cotangent[0]
    heads = HEADS // seq
    group = heads * HD
    hidden = w_gate.shape[1] // seq
    wrows = w_q.shape[0]

    def columns(weight):
        return lax.all_to_all(
            weight.reshape(wrows, seq, weight.shape[1] // seq), "seq", split_axis=1, concat_axis=0, tiled=False
        )

    def to_columns(weight):
        return columns(weight).reshape(seq, wrows, -1)

    gains = gather_small(jnp.stack([attn_gain, mlp_gain]), counts).astype(F32)
    gain_one, gain_two = gains[0], gains[1]

    out_weight = gather_rows(w_o[None], fsdp).reshape(group, width)
    qkv_piece = to_columns(
        jnp.concatenate([w.reshape(wrows, seq, group) for w in (w_q, w_k, w_v)], -1).reshape(wrows, -1)
    )
    qkv_weight = gather_rows(qkv_piece, fsdp).reshape(width, 3 * group)
    gate_weight = gather_rows(to_columns(w_gate), fsdp).reshape(width, hidden)
    up_weight = gather_rows(to_columns(w_up), fsdp).reshape(width, hidden)
    down_weight = gather_rows(w_down[None], fsdp).reshape(hidden, width)

    places = token_places(seq, rows)
    cosine, sine = rotary_tables(places)
    scale_one = rms_scale(inputs)
    normal_one = inputs * scale_one
    normed_one = gather_tokens((normal_one * gain_one).astype(LOW), seq)
    grad_out = gather_tokens(own_grad, seq)

    length = 2 * size
    qkv = jnp.concatenate(
        [jnp.dot(h, qkv_weight, preferred_element_type=F32) for h in normed_one], 0
    )
    heads_shape = (length, heads, HD)
    queries = rotary(qkv[:, :group].reshape(heads_shape), cosine, sine).astype(LOW).reshape(length, group)
    keys_all = (
        rotary(qkv[:, group : 2 * group].reshape(heads_shape), cosine, sine).astype(LOW).reshape(length, group)
    )
    values = qkv[:, 2 * group :].astype(LOW)
    attended, log_totals = attend_forward(queries, keys_all, values, places)
    projected = reduce_tokens(
        lambda half, low, high: jnp.dot(
            attended[half * size + low : half * size + high], out_weight, preferred_element_type=F32
        ),
        size,
        seq,
    )
    middle = inputs + projected
    scale_two = rms_scale(middle)
    normal_two = middle * scale_two
    normed_two = gather_tokens((normal_two * gain_two).astype(LOW), seq)
    mixed, grad_gate, grad_up = [], [], []
    for half in (0, 1):
        gate = jnp.dot(normed_two[half], gate_weight, preferred_element_type=F32)
        up = jnp.dot(normed_two[half], up_weight, preferred_element_type=F32)
        sigmoid = jax.nn.sigmoid(gate)
        silu = gate * sigmoid
        mixed.append((silu * up).astype(LOW))
        grad_mixed = jnp.einsum("td,fd->tf", grad_out[half], down_weight, preferred_element_type=F32)
        grad_gate.append(
            (grad_mixed * up * sigmoid * (1.0 + gate * (1.0 - sigmoid))).astype(LOW)
        )
        grad_up.append((grad_mixed * silu).astype(LOW))
    down_sum = reduce_tokens(
        lambda half, low, high: jnp.dot(mixed[half][low:high], down_weight, preferred_element_type=F32),
        size,
        seq,
    )
    layer_out = (middle + down_sum).astype(LOW)[None]
    grad_normed = reduce_tokens(
        lambda half, low, high: jnp.einsum(
            "tf,df->td", grad_gate[half][low:high], gate_weight, preferred_element_type=F32
        )
        + jnp.einsum("tf,df->td", grad_up[half][low:high], up_weight, preferred_element_type=F32),
        size,
        seq,
    )
    mixed, grad_gate, grad_up, normed_one, normed_two, grad_out = (
        jnp.concatenate(pair, 0) for pair in (mixed, grad_gate, grad_up, normed_one, normed_two, grad_out)
    )

    def outer(left, right):
        return jnp.einsum("ti,to->io", left, right, preferred_element_type=F32).astype(LOW)

    def row_grad(left, right):
        whole = outer(left, right)
        return reduce_rows(whole.reshape(1, fsdp, -1, width), fsdp)[0]

    def column_grad(left, right):
        whole = outer(left, right)
        piece = reduce_rows(whole.reshape(seq, fsdp, wrows, -1), fsdp)
        swapped = lax.all_to_all(piece.astype(LOW), "seq", split_axis=0, concat_axis=1, tiled=False)
        return swapped.astype(F32)

    grad_down_w = row_grad(mixed, grad_out)
    grad_gate_w = column_grad(normed_two, grad_gate).reshape(wrows, -1)
    grad_up_w = column_grad(normed_two, grad_up).reshape(wrows, -1)
    gain_two_piece = jnp.sum(grad_normed * normal_two, axis=0)
    grad_two = grad_normed * gain_two
    grad_middle = own_grad.astype(F32) + scale_two * (
        grad_two - normal_two * jnp.mean(grad_two * normal_two, axis=-1, keepdims=True)
    )
    grad_proj = jnp.concatenate(gather_tokens(grad_middle.astype(LOW), seq), 0)
    grad_heads = jnp.einsum("to,io->ti", grad_proj, out_weight, preferred_element_type=F32).astype(LOW)
    grad_out_w = row_grad(attended, grad_proj)
    grad_query_rot, grad_key_rot, grad_values = attend_backward(
        queries, keys_all, values, grad_heads, log_totals, places
    )
    grad_queries = rotary_back(grad_query_rot.astype(F32).reshape(heads_shape), cosine, sine)
    grad_keys = rotary_back(grad_key_rot.astype(F32).reshape(heads_shape), cosine, sine)
    grad_qkv = jnp.concatenate(
        [
            grad_queries.astype(LOW).reshape(length, group),
            grad_keys.astype(LOW).reshape(length, group),
            grad_values,
        ],
        -1,
    )
    grad_qkv_w = column_grad(normed_one, grad_qkv)
    grad_normed = reduce_tokens(
        lambda half, low, high: jnp.einsum(
            "to,io->ti",
            grad_qkv[half * size + low : half * size + high],
            qkv_weight,
            preferred_element_type=F32,
        ),
        size,
        seq,
    )
    gain_one_piece = jnp.sum(grad_normed * normal_one, axis=0)
    grad_one = grad_normed * gain_one
    grad_inputs = grad_middle + scale_one * (
        grad_one - normal_one * jnp.mean(grad_one * normal_one, axis=-1, keepdims=True)
    )
    return (
        layer_out,
        grad_inputs.astype(LOW)[None],
        scatter_small(gain_one_piece, counts),
        scatter_small(gain_two_piece, counts),
        grad_qkv_w[:, :, :group].reshape(wrows, width),
        grad_qkv_w[:, :, group : 2 * group].reshape(wrows, width),
        grad_qkv_w[:, :, 2 * group :].reshape(wrows, width),
        grad_out_w,
        grad_gate_w,
        grad_up_w,
        grad_down_w,
    )


def solution(mesh):
    tokens = P("fsdp", "seq", None)
    vector = P(("seq", "fsdp"))
    matrix = P(("seq", "fsdp"), None)
    return jax.shard_map(
        functools.partial(per_device, dict(mesh.shape)),
        mesh=mesh,
        in_specs=(tokens, tokens, vector, vector) + (matrix,) * 7,
        out_specs=(tokens, tokens, vector, vector) + (matrix,) * 7,
        check_vma=False,
    )
```

```python
import functools

import jax
import jax.numpy as jnp
from jax import lax
from jax.experimental import pallas as pl
from jax.experimental.pallas import tpu as pltpu
from jax.sharding import PartitionSpec as P

HEADS = 32
HD = 64
PAIR = 2 * HD
LANES = 128
TILE = 256
NT = (((1,), (1,)), ((), ()))

EPS = 1e-05
THETA = 130000.0

F32 = jnp.float32
LOW = jnp.bfloat16


def rms_scale(values):
    return lax.rsqrt(jnp.mean(values * values, axis=-1, keepdims=True) + EPS)


def rotary_tables(length):
    halfway = HD // 2
    frequency = THETA ** (-(jnp.arange(halfway, dtype=F32) * 2.0) / HD)
    angles = jnp.arange(length, dtype=jnp.int32).astype(F32)[:, None] * frequency[None, :]
    cosine = jnp.cos(angles)
    sine = jnp.sin(angles)
    return (
        jnp.concatenate([cosine, cosine, cosine, cosine], -1),
        jnp.concatenate([-sine, sine, -sine, sine], -1),
    )


def head_lanes(head):
    lane = lax.broadcasted_iota(jnp.int32, (1, PAIR), 1)
    return (lane >= head * HD) & (lane < (head + 1) * HD)


def half_turn(values):
    lane = lax.broadcasted_iota(jnp.int32, values.shape, 1)
    return jnp.where(
        lane % HD < HD // 2,
        pltpu.roll(values, PAIR - HD // 2, 1),
        pltpu.roll(values, HD // 2, 1),
    )


def causal(shape):
    return lax.broadcasted_iota(jnp.int32, shape, 0) <= lax.broadcasted_iota(jnp.int32, shape, 1)


def attend_kernel(
    block, order, q, k, v, cos, sin, q_out, k_out, v_out, o_out, log_out,
    v_turn, o_turn, o_flat, scores,
):
    length = q_out.shape[0]
    count = length // block
    for b in range(count):
        here = slice(b * block, (b + 1) * block)
        there = pl.ds(pl.multiple_of(order[b] * block, block), block)
        c, s = cos[there, :], sin[there, :]
        u = q[here, :]
        q_out[there, :] = (u * c + half_turn(u) * s).astype(LOW)
        u = k[here, :]
        k_out[there, :] = (u * c + half_turn(u) * s).astype(LOW)
        v_out[there, :] = v[here, :].astype(LOW)
    v_turn[...] = v_out[...].astype(F32).T.astype(LOW)
    for i in range(length // TILE):
        queries = q_out[i * TILE : (i + 1) * TILE, :] * HD ** (-0.5)
        for head in range(2):
            mine = jnp.where(head_lanes(head), queries, 0).astype(LOW)
            rows = slice(head * HD, (head + 1) * HD)
            highest = None
            for j in range(i + 1):
                part = lax.dot_general(
                    k_out[j * TILE : (j + 1) * TILE, :], mine, NT, preferred_element_type=F32
                )
                if i == j:
                    part = jnp.where(causal(part.shape), part, -1e30)
                scores[head, j * TILE : (j + 1) * TILE, :] = part
                top = jnp.max(part, axis=0, keepdims=True)
                highest = top if highest is None else jnp.maximum(highest, top)
            total = jnp.zeros((1, TILE), F32)
            acc = jnp.zeros((HD, TILE), F32)
            for j in range(i + 1):
                weights = jnp.exp(scores[head, j * TILE : (j + 1) * TILE, :] - highest)
                total += jnp.sum(weights, axis=0, keepdims=True)
                acc += jnp.dot(
                    v_turn[rows, j * TILE : (j + 1) * TILE], weights.astype(LOW), preferred_element_type=F32
                )
            o_turn[rows, i * TILE : (i + 1) * TILE] = acc / total
            log_out[0, head : head + 1, i * TILE : (i + 1) * TILE] = highest + jnp.log(total)
    o_flat[...] = o_turn[...].T
    for b in range(count):
        there = pl.ds(pl.multiple_of(order[b] * block, block), block)
        o_out[b * block : (b + 1) * block, :] = o_flat[there, :].astype(LOW)


def attend_forward(qkv, order, cos, sin, block):
    length, group = qkv.shape[0], qkv.shape[1] // 3
    pairs = group // PAIR

    def column(which):
        return pl.BlockSpec((length, PAIR), lambda p, order: (0, which * pairs + p))

    whole = pl.BlockSpec((length, PAIR), lambda p, order: (0, p))
    table = pl.BlockSpec((length, PAIR), lambda p, order: (0, 0))
    low = jax.ShapeDtypeStruct((length, group), LOW)
    return pl.pallas_call(
        functools.partial(attend_kernel, block),
        grid_spec=pltpu.PrefetchScalarGridSpec(
            num_scalar_prefetch=1,
            grid=(pairs,),
            in_specs=[column(0), column(1), column(2), table, table],
            out_specs=[whole] * 4 + [pl.BlockSpec((1, 2, length), lambda p, order: (p, 0, 0))],
            scratch_shapes=[
                pltpu.VMEM((PAIR, length), LOW),
                pltpu.VMEM((PAIR, length), F32),
                pltpu.VMEM((length, PAIR), F32),
                pltpu.VMEM((2, length, TILE), F32),
            ],
        ),
        out_shape=[low] * 4 + [jax.ShapeDtypeStruct((pairs, 2, length), F32)],
        compiler_params=pltpu.CompilerParams(vmem_limit_bytes=50 << 20),
        name="attend_forward",
    )(order, qkv, qkv, qkv, cos, sin)


def attend_back_kernel(
    block, order, q, k, v, o, grad, log, cos, sin, dq_out, dk_out, dv_out,
    do, k_turn, delta, dk, dv, dq_turn, flat,
):
    length = q.shape[0]
    count = length // block
    for b in range(count):
        here = slice(b * block, (b + 1) * block)
        there = pl.ds(pl.multiple_of(order[b] * block, block), block)
        do[there, :] = grad[here, :]
        flat[there, :] = grad[here, :].astype(F32) * o[here, :].astype(F32)
    turned = flat[...].T
    for head in range(2):
        delta[head : head + 1, :] = jnp.sum(turned[head * HD : (head + 1) * HD], axis=0, keepdims=True)
    k_turn[...] = k[...].astype(F32).T.astype(LOW)
    dk[...] = jnp.zeros_like(dk)
    dv[...] = jnp.zeros_like(dv)
    for i in range(length // TILE):
        span = slice(i * TILE, (i + 1) * TILE)
        queries = q[span, :] * HD ** (-0.5)
        for head in range(2):
            lanes = head_lanes(head)
            rows = slice(head * HD, (head + 1) * HD)
            mine = jnp.where(lanes, queries, 0).astype(LOW)
            mine_do = jnp.where(lanes, do[span, :], 0).astype(LOW)
            log_here = log[0, head : head + 1, span]
            delta_here = delta[head : head + 1, span]
            acc = jnp.zeros((HD, TILE), F32)
            for j in range(i + 1):
                keys = slice(j * TILE, (j + 1) * TILE)
                part = lax.dot_general(k[keys, :], mine, NT, preferred_element_type=F32)
                probs = jnp.exp(part - log_here)
                if i == j:
                    probs = jnp.where(causal(part.shape), probs, 0.0)
                d_probs = lax.dot_general(v[keys, :], mine_do, NT, preferred_element_type=F32)
                d_scores = (probs * (d_probs - delta_here)).astype(LOW)
                dv[keys, :] += jnp.dot(probs.astype(LOW), mine_do, preferred_element_type=F32)
                dk[keys, :] += jnp.dot(d_scores, mine, preferred_element_type=F32)
                acc += jnp.dot(k_turn[rows, keys], d_scores, preferred_element_type=F32)
            dq_turn[rows, span] = acc * HD ** (-0.5)
    flat[...] = dq_turn[...].T
    for b in range(count):
        here = slice(b * block, (b + 1) * block)
        there = pl.ds(pl.multiple_of(order[b] * block, block), block)
        c, s = cos[there, :], sin[there, :]
        u = flat[there, :].astype(LOW).astype(F32)
        dq_out[here, :] = (u * c - half_turn(u) * s).astype(LOW)
        u = dk[there, :].astype(LOW).astype(F32)
        dk_out[here, :] = (u * c - half_turn(u) * s).astype(LOW)
        dv_out[here, :] = dv[there, :].astype(LOW)


def attend_backward(q, k, v, o, grad, log, order, cos, sin, block):
    length, group = q.shape
    pairs = group // PAIR
    whole = pl.BlockSpec((length, PAIR), lambda p, order: (0, p))
    table = pl.BlockSpec((length, PAIR), lambda p, order: (0, 0))
    low = jax.ShapeDtypeStruct((length, group), LOW)
    return pl.pallas_call(
        functools.partial(attend_back_kernel, block),
        grid_spec=pltpu.PrefetchScalarGridSpec(
            num_scalar_prefetch=1,
            grid=(pairs,),
            in_specs=[whole] * 5 + [pl.BlockSpec((1, 2, length), lambda p, order: (p, 0, 0)), table, table],
            out_specs=[whole] * 3,
            scratch_shapes=[
                pltpu.VMEM((length, PAIR), LOW),
                pltpu.VMEM((PAIR, length), LOW),
                pltpu.VMEM((2, length), F32),
                pltpu.VMEM((length, PAIR), F32),
                pltpu.VMEM((length, PAIR), F32),
                pltpu.VMEM((PAIR, length), F32),
                pltpu.VMEM((length, PAIR), F32),
            ],
        ),
        out_shape=[low] * 3,
        compiler_params=pltpu.CompilerParams(vmem_limit_bytes=50 << 20),
        name="attend_backward",
    )(order, q, k, v, o, grad, log, cos, sin)


def pieces_of(width, seq, fsdp):
    piece = width // (seq * fsdp)
    for i in range(seq):
        for j in range(fsdp):
            here, there = i * fsdp + j, j * seq + i
            yield slice(here * piece, (here + 1) * piece), slice(there * piece, (there + 1) * piece)


def norm_kernel(seq, fsdp, which, gains, tokens, *refs):
    if which:
        terms, (middle, normed, flat) = refs[:-3], refs[-3:]
        block = terms[0].shape[0]
        each = len(terms) // 2
        for half in range(2):
            rows = slice(half * block, (half + 1) * block)
            total = tokens[rows, :].astype(F32)
            for term in terms[half * each : (half + 1) * each]:
                total = total + term[...].astype(F32)
            middle[rows, :] = total
        values = middle[...]
    else:
        normed, flat = refs
        values = tokens[...].astype(F32)
    normal = values * rms_scale(values)
    for here, there in pieces_of(normal.shape[1], seq, fsdp):
        flat[:, there] = normal[:, here]
    normed[...] = (flat[...] * gains[which : which + 1, :].astype(F32)).astype(LOW)


def norm_back_kernel(seq, fsdp, which, gains, source, straight, *refs):
    count = len([r for r in refs if r.shape[0] * 2 == source.shape[0]])
    terms, outs, (flat, sums) = refs[:count], refs[count:-2], refs[-2:]
    block = terms[0].shape[0]
    each = count // 2
    for half in range(2):
        total = None
        for term in terms[half * each : (half + 1) * each]:
            total = term[...].astype(F32) if total is None else total + term[...].astype(F32)
        sums[half * block : (half + 1) * block, :] = total * gains[which : which + 1, :].astype(F32)
    for here, there in pieces_of(source.shape[1], seq, fsdp):
        flat[:, here] = sums[:, there]
    values = source[...].astype(F32)
    scale = rms_scale(values)
    normal = values * scale
    grad = flat[...]
    total = straight[...].astype(F32) + scale * (
        grad - normal * jnp.mean(grad * normal, axis=-1, keepdims=True)
    )
    for out in outs:
        out[...] = total.astype(out.dtype)


def norm_call(kernel, name, counts, which, gains, args, sums, outs, steps=1):
    size, width = args[0].shape
    rows = size // steps
    whole = pl.BlockSpec((rows, width), lambda i: (i, 0))
    half = pl.BlockSpec((rows // 2, width), lambda i: (0, 0))
    flat = pltpu.VMEM((rows, width), F32)
    return pl.pallas_call(
        functools.partial(kernel, counts["seq"], counts["fsdp"], which),
        grid=(steps,),
        in_specs=[pl.BlockSpec(gains.shape, lambda i: (0, 0))] + [whole] * len(args) + [half] * len(sums),
        out_specs=[whole] * len(outs),
        out_shape=[jax.ShapeDtypeStruct((size, width), dtype) for dtype in outs],
        scratch_shapes=[flat] if kernel is norm_kernel else [flat, flat],
        compiler_params=pltpu.CompilerParams(vmem_limit_bytes=40 << 20),
        name=name,
    )(gains, *args, *sums)


def flip(values, axis, count, mask):
    return lax.ppermute(values, axis, [(i, i ^ mask) for i in range(count)])


def bits_of(count):
    return list(range(count.bit_length() - 1))


def token_bits(count, half):
    bits = bits_of(count)
    return bits[:1] + (bits[1:] if half == 0 else bits[:0:-1])


def by_core(parts):
    middle = len(parts[0]) // 2
    return parts[0][:middle] + parts[1][:middle] + parts[0][middle:] + parts[1][middle:]


def token_order(count):
    me = lax.axis_index("seq")
    parts = []
    for half in (0, 1):
        ranks = [0]
        for bit in reversed(token_bits(count, half)):
            ranks = ranks + [rank ^ (1 << bit) for rank in ranks]
        parts.append([(me ^ rank) * 2 + half for rank in ranks])
    return jnp.stack(by_core(parts)).astype(jnp.int32)


def after(values, *others):
    return lax.optimization_barrier((values,) + others)[0]


def gather_tokens(values, count):
    rows = values.shape[0] // 2
    parts = []
    for half in (0, 1):
        part = [values[half * rows : (half + 1) * rows]]
        for bit in reversed(token_bits(count, half)):
            part = part + [flip(block, "seq", count, 1 << bit) for block in part]
        parts.append(part)
    return jnp.concatenate(by_core(parts), 0)


def reduce_tokens(values, weight, dims, count, pins=(), parts=1):
    size = values.shape[0] // 2

    def part(rows):
        return lax.dot_general(rows, weight, (dims, ((), ())), preferred_element_type=F32)

    def pinned(step, got, kept):
        return pins[step](got, kept) if step < len(pins) and pins[step] else got

    rows = size // parts
    got = [
        flip(part(values[size + i * rows : size + (i + 1) * rows]).astype(LOW), "seq", count, 1)
        for i in range(parts)
    ]
    kept = [part(values[i * rows : (i + 1) * rows]) for i in range(parts)]
    kept = [k + g.astype(F32) for k, g in zip(kept, pinned(0, got, kept))]
    if parts == 1:
        kept = [kept[0][: size // 2], kept[0][size // 2 :]]
    for step in range(1, count.bit_length() - 1):
        got = []
        for half in (0, 1):
            middle = kept[half].shape[0] // 2
            sent = kept[half][middle:].astype(LOW)
            kept[half] = kept[half][:middle]
            got.append(flip(sent, "seq", count, 1 << token_bits(count, half)[step]))
        got = pinned(step, got, kept)
        if step < count.bit_length() - 2:
            kept = [k + g.astype(F32) for k, g in zip(kept, got)]
    return [kept[0], got[0], kept[1], got[1]]


def per_device(
    counts, tokens, cotangent, attn_gain, mlp_gain, w_q, w_k, w_v, w_o, w_gate, w_up, w_down
):
    seq, fsdp = counts["seq"], counts["fsdp"]
    rows = tokens.shape[1]
    width = tokens.shape[2]
    block = rows // 2
    length = rows * seq
    own_tokens = tokens[0]
    own_grad = cotangent[0]
    group = HEADS // seq * HD
    hidden = w_gate.shape[1] // seq
    wrows = w_q.shape[0]
    def swap(*weights):
        piece = jnp.concatenate([w.reshape(wrows, seq, -1) for w in weights], -1)
        return lax.all_to_all(piece, "seq", split_axis=1, concat_axis=0, tiled=True).reshape(seq * wrows, -1)

    def swap_back(piece):
        return lax.all_to_all(
            piece.reshape(seq, wrows, -1), "seq", split_axis=0, concat_axis=1, tiled=False
        )

    def gathered(piece):
        return lax.all_gather(piece, "fsdp", axis=0, tiled=True)

    def summed(whole):
        return lax.psum_scatter(whole, "fsdp", scatter_dimension=0, tiled=True)

    def outer(left, right):
        return jnp.einsum("ti,to->io", left, right, preferred_element_type=F32).astype(LOW)

    near = jnp.zeros((wrows, LANES), LOW).at[:, 0].set(attn_gain).at[:, 1].set(mlp_gain)
    near = jnp.broadcast_to(near[:, None], (wrows, seq, LANES)).reshape(wrows, seq * LANES)
    qkv_piece = swap(w_q, w_k, w_v, near)
    pair_piece = swap(after(w_gate, qkv_piece), w_up)
    first = gathered(jnp.concatenate([qkv_piece, w_o.reshape(seq * wrows, group)], -1))
    qkv_weight = first[:, : 3 * group]
    gains = first[:, 3 * group : 3 * group + 2].T
    out_weight = first[:, 3 * group + LANES :].reshape(group, width)
    pair_weight = gathered(after(pair_piece, first))
    down_weight = gathered(after(w_down, pair_weight))

    (normed_one,) = norm_call(
        norm_kernel, "norm_one", counts, 0, gains, [after(gather_tokens(own_tokens, seq), pair_piece)], [], [LOW], seq
    )
    order = token_order(seq)
    cosine, sine = rotary_tables(length)
    qkv = jnp.dot(normed_one, qkv_weight, preferred_element_type=F32)
    queries, keys, values, attended, logs = attend_forward(qkv, order, cosine, sine, block)
    sums = reduce_tokens(attended, out_weight, ((1,), (0,)), seq, parts=2)
    middle, own_two = norm_call(
        norm_kernel, "norm_two", counts, 1, gains, [own_tokens], sums, [F32, LOW]
    )
    normed_two = gather_tokens(own_two, seq)
    grad_out = gather_tokens(after(own_grad, normed_two, pair_weight), seq)
    gates = jnp.dot(normed_two, pair_weight, preferred_element_type=F32)
    gate, up = gates[:, :hidden], gates[:, hidden:]
    sigmoid = jax.nn.sigmoid(gate)
    mixed = (gate * sigmoid * up).astype(LOW)
    down_whole = outer(mixed, grad_out)
    down_part = summed(down_whole)
    grad_mixed = jnp.einsum(
        "td,fd->tf", after(grad_out, down_whole), down_weight, preferred_element_type=F32
    )
    grad_gate = (grad_mixed * up * sigmoid * (1.0 + gate * (1.0 - sigmoid))).astype(LOW)
    grad_up = (grad_mixed * gate * sigmoid).astype(LOW)
    grad_pair = jnp.concatenate([grad_gate, grad_up], -1)
    pair_whole = []

    def beside_pair(got, kept):
        pair_whole.append(outer(normed_two, after(grad_pair, *kept)))
        return got

    def after_pair(got, kept):
        return [after(g, pair_whole[0]) for g in got]

    sums = reduce_tokens(grad_pair, pair_weight, ((1,), (1,)), seq, [beside_pair, after_pair])
    pair_part = summed(after(pair_whole[0], down_part))
    grad_middle, own_proj = norm_call(
        norm_back_kernel, "norm_two_back", counts, 1, gains, [middle, own_grad], sums, [F32, LOW]
    )
    grad_proj = gather_tokens(own_proj, seq)

    out_whole = outer(attended, grad_proj)
    marks = []

    def hold(got, kept):
        marks.extend(kept)
        return [after(g, grad_proj) for g in got]

    def ahead(got, kept):
        marks.extend(got)
        return got

    down = reduce_tokens(after(mixed, own_proj), down_weight, ((1,), (0,)), seq, [hold, ahead])
    down_sum = jnp.concatenate([down[0] + down[1].astype(F32), down[2] + down[3].astype(F32)], 0)
    layer_out = (middle + down_sum).astype(LOW)[None]
    grad_heads = jnp.einsum(
        "to,io->ti", after(grad_proj, marks[0]), out_weight, preferred_element_type=F32
    ).astype(LOW)
    grad_qkv = jnp.concatenate(
        attend_backward(queries, keys, values, attended, grad_heads, logs, order, cosine, sine, block), -1
    )
    qkv_whole = outer(normed_one, after(grad_qkv, *marks[1:]))
    sums = reduce_tokens(after(grad_qkv, qkv_whole), qkv_weight, ((1,), (1,)), seq)
    (grad_inputs,) = norm_call(
        norm_back_kernel, "norm_one_back", counts, 0, gains, [own_tokens, grad_middle], sums, [LOW]
    )
    last_whole = jnp.concatenate([qkv_whole, out_whole.reshape(width, group)], -1)
    last_part = summed(after(last_whole, pair_part))
    qkv_part, out_part = last_part[:, : 3 * group], last_part[:, 3 * group :].reshape(wrows, width)

    def finish(piece, weight):
        piece = piece.reshape(wrows, -1).astype(F32)
        return piece, jnp.sum(piece * weight.astype(F32), axis=-1)

    pair_near = swap_back(pair_part)
    grad_gate_w, gate_gain = finish(pair_near[:, :, :hidden], w_gate)
    grad_up_w, up_gain = finish(pair_near[:, :, hidden:], w_up)
    qkv_near = swap_back(qkv_part)
    grad_q_w, q_gain = finish(qkv_near[:, :, :group], w_q)
    grad_k_w, k_gain = finish(qkv_near[:, :, group : 2 * group], w_k)
    grad_v_w, v_gain = finish(qkv_near[:, :, 2 * group :], w_v)
    return (
        layer_out,
        grad_inputs[None],
        (q_gain + k_gain + v_gain) / attn_gain.astype(F32),
        (gate_gain + up_gain) / mlp_gain.astype(F32),
        grad_q_w,
        grad_k_w,
        grad_v_w,
        out_part.astype(F32),
        grad_gate_w,
        grad_up_w,
        down_part.astype(F32),
    )


def solution(mesh):
    tokens = P("fsdp", "seq", None)
    vector = P(("seq", "fsdp"))
    matrix = P(("seq", "fsdp"), None)
    return jax.shard_map(
        functools.partial(per_device, dict(mesh.shape)),
        mesh=mesh,
        in_specs=(tokens, tokens, vector, vector) + (matrix,) * 7,
        out_specs=(tokens, tokens, vector, vector) + (matrix,) * 7,
        check_vma=False,
    )
```

```python
import functools

import jax
import jax.numpy as jnp
from jax import lax
from jax.experimental import pallas as pl
from jax.experimental.pallas import tpu as pltpu
from jax.sharding import PartitionSpec as P

HEADS = 32
HD = 64
PAIR = 2 * HD
LANES = 128
GAIN_ROWS = 16
TILE = 256
NT = (((1,), (1,)), ((), ()))

EPS = 1e-05
THETA = 130000.0

F32 = jnp.float32
LOW = jnp.bfloat16


def rms_scale(values):
    return lax.rsqrt(jnp.mean(values * values, axis=-1, keepdims=True) + EPS)


def rotary_tables(length):
    halfway = HD // 2
    frequency = THETA ** (-(jnp.arange(halfway, dtype=F32) * 2.0) / HD)
    angles = jnp.arange(length, dtype=jnp.int32).astype(F32)[:, None] * frequency[None, :]
    cosine = jnp.cos(angles)
    sine = jnp.sin(angles)
    return (
        jnp.concatenate([cosine, cosine, cosine, cosine], -1),
        jnp.concatenate([-sine, sine, -sine, sine], -1),
    )


def head_lanes(head):
    lane = lax.broadcasted_iota(jnp.int32, (1, PAIR), 1)
    return (lane >= head * HD) & (lane < (head + 1) * HD)


def half_turn(values):
    lane = lax.broadcasted_iota(jnp.int32, values.shape, 1)
    return jnp.where(
        lane % HD < HD // 2,
        pltpu.roll(values, PAIR - HD // 2, 1),
        pltpu.roll(values, HD // 2, 1),
    )


def causal(shape):
    return lax.broadcasted_iota(jnp.int32, shape, 0) <= lax.broadcasted_iota(jnp.int32, shape, 1)


def attend_kernel(
    block, order, q, k, v, cos, sin, q_out, k_out, v_out, o_out, log_out,
    v_turn, o_turn, o_flat, scores,
):
    length = q_out.shape[0]
    count = length // block
    for b in range(count):
        here = slice(b * block, (b + 1) * block)
        there = pl.ds(pl.multiple_of(order[b] * block, block), block)
        c, s = cos[there, :], sin[there, :]
        u = q[here, :]
        q_out[there, :] = (u * c + half_turn(u) * s).astype(LOW)
        u = k[here, :]
        k_out[there, :] = (u * c + half_turn(u) * s).astype(LOW)
        v_out[there, :] = v[here, :].astype(LOW)
    v_turn[...] = v_out[...].astype(F32).T.astype(LOW)
    for i in range(length // TILE):
        queries = q_out[i * TILE : (i + 1) * TILE, :] * HD ** (-0.5)
        for head in range(2):
            mine = jnp.where(head_lanes(head), queries, 0).astype(LOW)
            rows = slice(head * HD, (head + 1) * HD)
            highest = None
            for j in range(i + 1):
                part = lax.dot_general(
                    k_out[j * TILE : (j + 1) * TILE, :], mine, NT, preferred_element_type=F32
                )
                if i == j:
                    part = jnp.where(causal(part.shape), part, -1e30)
                scores[head, j * TILE : (j + 1) * TILE, :] = part
                top = jnp.max(part, axis=0, keepdims=True)
                highest = top if highest is None else jnp.maximum(highest, top)
            total = jnp.zeros((1, TILE), F32)
            acc = jnp.zeros((HD, TILE), F32)
            for j in range(i + 1):
                weights = jnp.exp(scores[head, j * TILE : (j + 1) * TILE, :] - highest)
                total += jnp.sum(weights, axis=0, keepdims=True)
                acc += jnp.dot(
                    v_turn[rows, j * TILE : (j + 1) * TILE], weights.astype(LOW), preferred_element_type=F32
                )
            o_turn[rows, i * TILE : (i + 1) * TILE] = acc / total
            log_out[0, head : head + 1, i * TILE : (i + 1) * TILE] = highest + jnp.log(total)
    o_flat[...] = o_turn[...].T
    for b in range(count):
        there = pl.ds(pl.multiple_of(order[b] * block, block), block)
        o_out[b * block : (b + 1) * block, :] = o_flat[there, :].astype(LOW)


def attend_forward(qkv, order, cos, sin, block):
    length, group = qkv.shape[0], qkv.shape[1] // 3
    pairs = group // PAIR

    def column(which):
        return pl.BlockSpec((length, PAIR), lambda p, order: (0, which * pairs + p))

    whole = pl.BlockSpec((length, PAIR), lambda p, order: (0, p))
    table = pl.BlockSpec((length, PAIR), lambda p, order: (0, 0))
    low = jax.ShapeDtypeStruct((length, group), LOW)
    return pl.pallas_call(
        functools.partial(attend_kernel, block),
        grid_spec=pltpu.PrefetchScalarGridSpec(
            num_scalar_prefetch=1,
            grid=(pairs,),
            in_specs=[column(0), column(1), column(2), table, table],
            out_specs=[whole] * 4 + [pl.BlockSpec((1, 2, length), lambda p, order: (p, 0, 0))],
            scratch_shapes=[
                pltpu.VMEM((PAIR, length), LOW),
                pltpu.VMEM((PAIR, length), F32),
                pltpu.VMEM((length, PAIR), F32),
                pltpu.VMEM((2, length, TILE), F32),
            ],
        ),
        out_shape=[low] * 4 + [jax.ShapeDtypeStruct((pairs, 2, length), F32)],
        compiler_params=pltpu.CompilerParams(vmem_limit_bytes=50 << 20),
        name="attend_forward",
    )(order, qkv, qkv, qkv, cos, sin)


def attend_back_kernel(
    block, order, q, k, v, o, grad, log, cos, sin, dq_out, dk_out, dv_out,
    do, k_turn, delta, dk, dv, dq_turn, flat,
):
    length = q.shape[0]
    count = length // block
    for b in range(count):
        here = slice(b * block, (b + 1) * block)
        there = pl.ds(pl.multiple_of(order[b] * block, block), block)
        do[there, :] = grad[here, :]
        flat[there, :] = grad[here, :].astype(F32) * o[here, :].astype(F32)
    turned = flat[...].T
    for head in range(2):
        delta[head : head + 1, :] = jnp.sum(turned[head * HD : (head + 1) * HD], axis=0, keepdims=True)
    k_turn[...] = k[...].astype(F32).T.astype(LOW)
    dk[...] = jnp.zeros_like(dk)
    dv[...] = jnp.zeros_like(dv)
    for i in range(length // TILE):
        span = slice(i * TILE, (i + 1) * TILE)
        queries = q[span, :] * HD ** (-0.5)
        for head in range(2):
            lanes = head_lanes(head)
            rows = slice(head * HD, (head + 1) * HD)
            mine = jnp.where(lanes, queries, 0).astype(LOW)
            mine_do = jnp.where(lanes, do[span, :], 0).astype(LOW)
            log_here = log[0, head : head + 1, span]
            delta_here = delta[head : head + 1, span]
            acc = jnp.zeros((HD, TILE), F32)
            for j in range(i + 1):
                keys = slice(j * TILE, (j + 1) * TILE)
                part = lax.dot_general(k[keys, :], mine, NT, preferred_element_type=F32)
                probs = jnp.exp(part - log_here)
                if i == j:
                    probs = jnp.where(causal(part.shape), probs, 0.0)
                d_probs = lax.dot_general(v[keys, :], mine_do, NT, preferred_element_type=F32)
                d_scores = (probs * (d_probs - delta_here)).astype(LOW)
                dv[keys, :] += jnp.dot(probs.astype(LOW), mine_do, preferred_element_type=F32)
                dk[keys, :] += jnp.dot(d_scores, mine, preferred_element_type=F32)
                acc += jnp.dot(k_turn[rows, keys], d_scores, preferred_element_type=F32)
            dq_turn[rows, span] = acc * HD ** (-0.5)
    flat[...] = dq_turn[...].T
    for b in range(count):
        here = slice(b * block, (b + 1) * block)
        there = pl.ds(pl.multiple_of(order[b] * block, block), block)
        c, s = cos[there, :], sin[there, :]
        u = flat[there, :].astype(LOW).astype(F32)
        dq_out[here, :] = (u * c - half_turn(u) * s).astype(LOW)
        u = dk[there, :].astype(LOW).astype(F32)
        dk_out[here, :] = (u * c - half_turn(u) * s).astype(LOW)
        dv_out[here, :] = dv[there, :].astype(LOW)


def attend_backward(q, k, v, o, grad, log, order, cos, sin, block):
    length, group = q.shape
    pairs = group // PAIR
    whole = pl.BlockSpec((length, PAIR), lambda p, order: (0, p))
    table = pl.BlockSpec((length, PAIR), lambda p, order: (0, 0))
    low = jax.ShapeDtypeStruct((length, group), LOW)
    return pl.pallas_call(
        functools.partial(attend_back_kernel, block),
        grid_spec=pltpu.PrefetchScalarGridSpec(
            num_scalar_prefetch=1,
            grid=(pairs,),
            in_specs=[whole] * 5 + [pl.BlockSpec((1, 2, length), lambda p, order: (p, 0, 0)), table, table],
            out_specs=[whole] * 3,
            scratch_shapes=[
                pltpu.VMEM((length, PAIR), LOW),
                pltpu.VMEM((PAIR, length), LOW),
                pltpu.VMEM((2, length), F32),
                pltpu.VMEM((length, PAIR), F32),
                pltpu.VMEM((length, PAIR), F32),
                pltpu.VMEM((PAIR, length), F32),
                pltpu.VMEM((length, PAIR), F32),
            ],
        ),
        out_shape=[low] * 3,
        compiler_params=pltpu.CompilerParams(vmem_limit_bytes=50 << 20),
        name="attend_backward",
    )(order, q, k, v, o, grad, log, cos, sin)


def pieces_of(width, seq, fsdp):
    piece = width // (seq * fsdp)
    for i in range(seq):
        for j in range(fsdp):
            here, there = i * fsdp + j, j * seq + i
            yield slice(here * piece, (here + 1) * piece), slice(there * piece, (there + 1) * piece)


def norm_kernel(seq, fsdp, which, gains, tokens, *refs):
    if which:
        terms, (middle, normed, flat) = refs[:-3], refs[-3:]
        block = terms[0].shape[0]
        each = len(terms) // 2
        for half in range(2):
            rows = slice(half * block, (half + 1) * block)
            total = tokens[rows, :].astype(F32)
            for term in terms[half * each : (half + 1) * each]:
                total = total + term[...].astype(F32)
            middle[rows, :] = total
        values = middle[...]
    else:
        normed, flat = refs
        values = tokens[...].astype(F32)
    normal = values * rms_scale(values)
    for here, there in pieces_of(normal.shape[1], seq, fsdp):
        flat[:, there] = normal[:, here]
    normed[...] = (flat[...] * gains[which : which + 1, :].astype(F32)).astype(LOW)


def norm_back_kernel(seq, fsdp, which, gains, source, straight, *refs):
    count = len([r for r in refs if r.shape[0] * 2 == source.shape[0]])
    terms, outs, (flat, sums) = refs[:count], refs[count:-2], refs[-2:]
    block = terms[0].shape[0]
    each = count // 2
    for half in range(2):
        total = None
        for term in terms[half * each : (half + 1) * each]:
            total = term[...].astype(F32) if total is None else total + term[...].astype(F32)
        sums[half * block : (half + 1) * block, :] = total * gains[which : which + 1, :].astype(F32)
    for here, there in pieces_of(source.shape[1], seq, fsdp):
        flat[:, here] = sums[:, there]
    values = source[...].astype(F32)
    scale = rms_scale(values)
    normal = values * scale
    grad = flat[...]
    total = straight[...].astype(F32) + scale * (
        grad - normal * jnp.mean(grad * normal, axis=-1, keepdims=True)
    )
    for out in outs:
        out[...] = total.astype(out.dtype)


def norm_call(kernel, name, counts, which, gains, args, sums, outs, steps=1):
    size, width = args[0].shape
    rows = size // steps
    whole = pl.BlockSpec((rows, width), lambda i: (i, 0))
    half = pl.BlockSpec((rows // 2, width), lambda i: (0, 0))
    flat = pltpu.VMEM((rows, width), F32)
    return pl.pallas_call(
        functools.partial(kernel, counts["seq"], counts["fsdp"], which),
        grid=(steps,),
        in_specs=[pl.BlockSpec(gains.shape, lambda i: (0, 0))] + [whole] * len(args) + [half] * len(sums),
        out_specs=[whole] * len(outs),
        out_shape=[jax.ShapeDtypeStruct((size, width), dtype) for dtype in outs],
        scratch_shapes=[flat] if kernel is norm_kernel else [flat, flat],
        compiler_params=pltpu.CompilerParams(vmem_limit_bytes=40 << 20),
        name=name,
    )(gains, *args, *sums)


def flip(values, axis, count, mask):
    return lax.ppermute(values, axis, [(i, i ^ mask) for i in range(count)])


def bits_of(count):
    return list(range(count.bit_length() - 1))


def token_bits(count, half):
    bits = bits_of(count)
    return bits[:1] + (bits[1:] if half == 0 else bits[:0:-1])


def by_core(parts):
    middle = len(parts[0]) // 2
    return parts[0][:middle] + parts[1][:middle] + parts[0][middle:] + parts[1][middle:]


def token_order(count):
    me = lax.axis_index("seq")
    parts = []
    for half in (0, 1):
        ranks = [0]
        for bit in reversed(token_bits(count, half)):
            ranks = ranks + [rank ^ (1 << bit) for rank in ranks]
        parts.append([(me ^ rank) * 2 + half for rank in ranks])
    return jnp.stack(by_core(parts)).astype(jnp.int32)


def after(values, *others):
    return lax.optimization_barrier((values,) + others)[0]


def gather_tokens(values, count):
    rows = values.shape[0] // 2
    parts = []
    for half in (0, 1):
        part = [values[half * rows : (half + 1) * rows]]
        for bit in reversed(token_bits(count, half)):
            part = part + [flip(block, "seq", count, 1 << bit) for block in part]
        parts.append(part)
    return jnp.concatenate(by_core(parts), 0)


def reduce_tokens(values, weight, dims, count, pins=(), parts=1):
    size = values.shape[0] // 2

    def part(rows):
        return lax.dot_general(rows, weight, (dims, ((), ())), preferred_element_type=F32)

    def pinned(step, got, kept):
        return pins[step](got, kept) if step < len(pins) and pins[step] else got

    rows = size // parts
    got = [
        flip(part(values[size + i * rows : size + (i + 1) * rows]).astype(LOW), "seq", count, 1)
        for i in range(parts)
    ]
    kept = [part(values[i * rows : (i + 1) * rows]) for i in range(parts)]
    kept = [k + g.astype(F32) for k, g in zip(kept, pinned(0, got, kept))]
    if parts == 1:
        kept = [kept[0][: size // 2], kept[0][size // 2 :]]
    for step in range(1, count.bit_length() - 1):
        got = []
        for half in (0, 1):
            middle = kept[half].shape[0] // 2
            sent = kept[half][middle:].astype(LOW)
            kept[half] = kept[half][:middle]
            got.append(flip(sent, "seq", count, 1 << token_bits(count, half)[step]))
        got = pinned(step, got, kept)
        if step < count.bit_length() - 2:
            kept = [k + g.astype(F32) for k, g in zip(kept, got)]
    return [kept[0], got[0], kept[1], got[1]]


def per_device(
    counts, tokens, cotangent, attn_gain, mlp_gain, w_q, w_k, w_v, w_o, w_gate, w_up, w_down
):
    seq, fsdp = counts["seq"], counts["fsdp"]
    rows = tokens.shape[1]
    width = tokens.shape[2]
    block = rows // 2
    length = rows * seq
    own_tokens = tokens[0]
    own_grad = cotangent[0]
    group = HEADS // seq * HD
    hidden = w_gate.shape[1] // seq
    wrows = w_q.shape[0]
    def swap(*weights):
        piece = jnp.concatenate([w.reshape(wrows, seq, -1) for w in weights], -1)
        return lax.all_to_all(piece, "seq", split_axis=1, concat_axis=0, tiled=True).reshape(seq * wrows, -1)

    def swap_back(piece):
        return lax.all_to_all(
            piece.reshape(seq, wrows, -1), "seq", split_axis=0, concat_axis=1, tiled=False
        )

    def gathered(piece):
        return lax.all_gather(piece, "fsdp", axis=0, tiled=True)

    def summed(whole):
        return lax.psum_scatter(whole, "fsdp", scatter_dimension=0, tiled=True)

    def outer(left, right):
        return jnp.einsum("ti,to->io", left, right, preferred_element_type=F32).astype(LOW)

    near = jnp.zeros((wrows, LANES), LOW).at[:, 0].set(attn_gain).at[:, 1].set(mlp_gain)
    near = jnp.broadcast_to(near[:, None], (wrows, seq, LANES)).reshape(wrows, seq * LANES)
    qkv_piece = swap(w_q, w_k, w_v, near)
    pair_piece = swap(after(w_gate, qkv_piece), w_up)
    down_first = gathered(w_down[:, : width // 2])
    tall = seq * wrows
    wide = 4 * group
    piece = jnp.concatenate([qkv_piece[:, : 3 * group], w_o.reshape(tall, group)], -1)
    own_gains = qkv_piece[:, 3 * group : 3 * group + 2].T
    extra = GAIN_ROWS * -(-2 * tall // (GAIN_ROWS * wide))
    own_gains = jnp.pad(own_gains.reshape(-1), (0, extra * wide - 2 * tall)).reshape(extra, wide)
    first = gathered(after(jnp.concatenate([piece, own_gains], 0), down_first)).reshape(fsdp, tall + extra, wide)
    qkv_weight = first[:, :tall, : 3 * group].reshape(width, 3 * group)
    out_weight = first[:, :tall, 3 * group :].reshape(group, width)
    gains = first[:, tall:].reshape(fsdp, -1)[:, : 2 * tall].reshape(fsdp, 2, tall).swapaxes(0, 1).reshape(2, width)
    grad_out = gather_tokens(after(own_grad, pair_piece), seq)
    pair_weight = gathered(after(pair_piece, first, grad_out))
    down_last = gathered(after(w_down[:, width // 2 :], pair_weight))

    (normed_one,) = norm_call(
        norm_kernel, "norm_one", counts, 0, gains, [after(gather_tokens(own_tokens, seq), pair_piece)], [], [LOW], seq
    )
    order = token_order(seq)
    cosine, sine = rotary_tables(length)
    qkv = jnp.dot(normed_one, qkv_weight, preferred_element_type=F32)
    queries, keys, values, attended, logs = attend_forward(qkv, order, cosine, sine, block)
    sums = reduce_tokens(attended, out_weight, ((1,), (0,)), seq, parts=2)
    middle, own_two = norm_call(
        norm_kernel, "norm_two", counts, 1, gains, [own_tokens], sums, [F32, LOW]
    )
    normed_two = gather_tokens(own_two, seq)
    gates = jnp.dot(normed_two, pair_weight, preferred_element_type=F32)
    gate, up = gates[:, :hidden], gates[:, hidden:]
    sigmoid = jax.nn.sigmoid(gate)
    mixed = (gate * sigmoid * up).astype(LOW)
    down_whole = outer(mixed, grad_out)
    down_part = summed(after(down_whole, down_last))
    cot = after(grad_out, down_whole)
    grad_mixed = jnp.einsum(
        "td,fd->tf", cot[:, : width // 2], down_first, preferred_element_type=F32
    ) + jnp.einsum("td,fd->tf", cot[:, width // 2 :], down_last, preferred_element_type=F32)
    down_weight = jnp.concatenate([down_first, down_last], -1)
    grad_gate = (grad_mixed * up * sigmoid * (1.0 + gate * (1.0 - sigmoid))).astype(LOW)
    grad_up = (grad_mixed * gate * sigmoid).astype(LOW)
    grad_pair = jnp.concatenate([grad_gate, grad_up], -1)
    pair_whole = []

    def beside_pair(got, kept):
        pair_whole.append(outer(normed_two, after(grad_pair, *kept)))
        return got

    def after_pair(got, kept):
        return [after(g, pair_whole[0]) for g in got]

    sums = reduce_tokens(grad_pair, pair_weight, ((1,), (1,)), seq, [beside_pair, after_pair])
    pair_part = summed(after(pair_whole[0], down_part))
    grad_middle, own_proj = norm_call(
        norm_back_kernel, "norm_two_back", counts, 1, gains, [middle, own_grad], sums, [F32, LOW]
    )
    grad_proj = gather_tokens(own_proj, seq)

    out_whole = outer(attended, grad_proj)
    marks = []

    def hold(got, kept):
        marks.extend(kept)
        return [after(g, grad_proj) for g in got]

    def ahead(got, kept):
        marks.extend(got)
        return got

    down = reduce_tokens(after(mixed, own_proj), down_weight, ((1,), (0,)), seq, [hold, ahead])
    down_sum = jnp.concatenate([down[0] + down[1].astype(F32), down[2] + down[3].astype(F32)], 0)
    layer_out = (middle + down_sum).astype(LOW)[None]
    grad_heads = jnp.einsum(
        "to,io->ti", after(grad_proj, marks[0]), out_weight, preferred_element_type=F32
    ).astype(LOW)
    grad_qkv = jnp.concatenate(
        attend_backward(queries, keys, values, attended, grad_heads, logs, order, cosine, sine, block), -1
    )
    qkv_whole = outer(normed_one, after(grad_qkv, *marks[1:]))
    sums = reduce_tokens(after(grad_qkv, qkv_whole), qkv_weight, ((1,), (1,)), seq)
    (grad_inputs,) = norm_call(
        norm_back_kernel, "norm_one_back", counts, 0, gains, [own_tokens, grad_middle], sums, [LOW]
    )
    last_whole = jnp.concatenate([qkv_whole, out_whole.reshape(width, group)], -1)
    last_part = summed(after(last_whole, pair_part))
    qkv_part, out_part = last_part[:, : 3 * group], last_part[:, 3 * group :].reshape(wrows, width)

    def finish(piece, weight):
        piece = piece.reshape(wrows, -1).astype(F32)
        return piece, jnp.sum(piece * weight.astype(F32), axis=-1)

    pair_near = swap_back(pair_part)
    grad_gate_w, gate_gain = finish(pair_near[:, :, :hidden], w_gate)
    grad_up_w, up_gain = finish(pair_near[:, :, hidden:], w_up)
    qkv_near = swap_back(qkv_part)
    grad_q_w, q_gain = finish(qkv_near[:, :, :group], w_q)
    grad_k_w, k_gain = finish(qkv_near[:, :, group : 2 * group], w_k)
    grad_v_w, v_gain = finish(qkv_near[:, :, 2 * group :], w_v)
    return (
        layer_out,
        grad_inputs[None],
        (q_gain + k_gain + v_gain) / attn_gain.astype(F32),
        (gate_gain + up_gain) / mlp_gain.astype(F32),
        grad_q_w,
        grad_k_w,
        grad_v_w,
        out_part.astype(F32),
        grad_gate_w,
        grad_up_w,
        down_part.astype(F32),
    )


def solution(mesh):
    tokens = P("fsdp", "seq", None)
    vector = P(("seq", "fsdp"))
    matrix = P(("seq", "fsdp"), None)
    return jax.shard_map(
        functools.partial(per_device, dict(mesh.shape)),
        mesh=mesh,
        in_specs=(tokens, tokens, vector, vector) + (matrix,) * 7,
        out_specs=(tokens, tokens, vector, vector) + (matrix,) * 7,
        check_vma=False,
    )
```

```python
import functools

import jax
import jax.numpy as jnp
from jax import lax
from jax.experimental import pallas as pl
from jax.experimental.pallas import tpu as pltpu
from jax.sharding import PartitionSpec as P

HEADS = 32
HD = 64
PAIR = 2 * HD
LANES = 128
GAIN_ROWS = 16
TILE = 256
NT = (((1,), (1,)), ((), ()))

EPS = 1e-05
THETA = 130000.0

F32 = jnp.float32
LOW = jnp.bfloat16


def rms_scale(values):
    return lax.rsqrt(jnp.mean(values * values, axis=-1, keepdims=True) + EPS)


def rotary_tables(length):
    halfway = HD // 2
    frequency = THETA ** (-(jnp.arange(halfway, dtype=F32) * 2.0) / HD)
    angles = jnp.arange(length, dtype=jnp.int32).astype(F32)[:, None] * frequency[None, :]
    cosine = jnp.cos(angles)
    sine = jnp.sin(angles)
    return (
        jnp.concatenate([cosine, cosine, cosine, cosine], -1),
        jnp.concatenate([-sine, sine, -sine, sine], -1),
    )


def head_lanes(head):
    lane = lax.broadcasted_iota(jnp.int32, (1, PAIR), 1)
    return (lane >= head * HD) & (lane < (head + 1) * HD)


def half_turn(values):
    lane = lax.broadcasted_iota(jnp.int32, values.shape, 1)
    return jnp.where(
        lane % HD < HD // 2,
        pltpu.roll(values, PAIR - HD // 2, 1),
        pltpu.roll(values, HD // 2, 1),
    )


def causal(shape):
    return lax.broadcasted_iota(jnp.int32, shape, 0) <= lax.broadcasted_iota(jnp.int32, shape, 1)


def attend_kernel(
    block, order, q, k, v, cos, sin, q_out, k_out, v_out, o_out, log_out,
    v_turn, o_turn, o_flat, scores,
):
    length = q_out.shape[0]
    count = length // block
    for b in range(count):
        here = slice(b * block, (b + 1) * block)
        there = pl.ds(pl.multiple_of(order[b] * block, block), block)
        c, s = cos[there, :], sin[there, :]
        u = q[here, :]
        q_out[there, :] = (u * c + half_turn(u) * s).astype(LOW)
        u = k[here, :]
        k_out[there, :] = (u * c + half_turn(u) * s).astype(LOW)
        v_out[there, :] = v[here, :].astype(LOW)
    v_turn[...] = v_out[...].astype(F32).T.astype(LOW)
    for i in range(length // TILE):
        queries = q_out[i * TILE : (i + 1) * TILE, :] * HD ** (-0.5)
        for head in range(2):
            mine = jnp.where(head_lanes(head), queries, 0).astype(LOW)
            rows = slice(head * HD, (head + 1) * HD)
            highest = None
            for j in range(i + 1):
                part = lax.dot_general(
                    k_out[j * TILE : (j + 1) * TILE, :], mine, NT, preferred_element_type=F32
                )
                if i == j:
                    part = jnp.where(causal(part.shape), part, -1e30)
                scores[head, j * TILE : (j + 1) * TILE, :] = part
                top = jnp.max(part, axis=0, keepdims=True)
                highest = top if highest is None else jnp.maximum(highest, top)
            total = jnp.zeros((1, TILE), F32)
            acc = jnp.zeros((HD, TILE), F32)
            for j in range(i + 1):
                weights = jnp.exp(scores[head, j * TILE : (j + 1) * TILE, :] - highest)
                total += jnp.sum(weights, axis=0, keepdims=True)
                acc += jnp.dot(
                    v_turn[rows, j * TILE : (j + 1) * TILE], weights.astype(LOW), preferred_element_type=F32
                )
            o_turn[rows, i * TILE : (i + 1) * TILE] = acc / total
            log_out[0, head : head + 1, i * TILE : (i + 1) * TILE] = highest + jnp.log(total)
    o_flat[...] = o_turn[...].T
    for b in range(count):
        there = pl.ds(pl.multiple_of(order[b] * block, block), block)
        o_out[b * block : (b + 1) * block, :] = o_flat[there, :].astype(LOW)


def attend_forward(qkv, order, cos, sin, block):
    length, group = qkv.shape[0], qkv.shape[1] // 3
    pairs = group // PAIR

    def column(which):
        return pl.BlockSpec((length, PAIR), lambda p, order: (0, which * pairs + p))

    whole = pl.BlockSpec((length, PAIR), lambda p, order: (0, p))
    table = pl.BlockSpec((length, PAIR), lambda p, order: (0, 0))
    low = jax.ShapeDtypeStruct((length, group), LOW)
    return pl.pallas_call(
        functools.partial(attend_kernel, block),
        grid_spec=pltpu.PrefetchScalarGridSpec(
            num_scalar_prefetch=1,
            grid=(pairs,),
            in_specs=[column(0), column(1), column(2), table, table],
            out_specs=[whole] * 4 + [pl.BlockSpec((1, 2, length), lambda p, order: (p, 0, 0))],
            scratch_shapes=[
                pltpu.VMEM((PAIR, length), LOW),
                pltpu.VMEM((PAIR, length), F32),
                pltpu.VMEM((length, PAIR), F32),
                pltpu.VMEM((2, length, TILE), F32),
            ],
        ),
        out_shape=[low] * 4 + [jax.ShapeDtypeStruct((pairs, 2, length), F32)],
        compiler_params=pltpu.CompilerParams(vmem_limit_bytes=50 << 20),
        name="attend_forward",
    )(order, qkv, qkv, qkv, cos, sin)


def attend_back_kernel(
    block, order, q, k, v, o, grad, log, cos, sin, dq_out, dk_out, dv_out,
    do, k_turn, delta, dk, dv, dq_turn, flat,
):
    length = q.shape[0]
    count = length // block
    for b in range(count):
        here = slice(b * block, (b + 1) * block)
        there = pl.ds(pl.multiple_of(order[b] * block, block), block)
        do[there, :] = grad[here, :]
        flat[there, :] = grad[here, :].astype(F32) * o[here, :].astype(F32)
    turned = flat[...].T
    for head in range(2):
        delta[head : head + 1, :] = jnp.sum(turned[head * HD : (head + 1) * HD], axis=0, keepdims=True)
    k_turn[...] = k[...].astype(F32).T.astype(LOW)
    dk[...] = jnp.zeros_like(dk)
    dv[...] = jnp.zeros_like(dv)
    for i in range(length // TILE):
        span = slice(i * TILE, (i + 1) * TILE)
        queries = q[span, :] * HD ** (-0.5)
        for head in range(2):
            lanes = head_lanes(head)
            rows = slice(head * HD, (head + 1) * HD)
            mine = jnp.where(lanes, queries, 0).astype(LOW)
            mine_do = jnp.where(lanes, do[span, :], 0).astype(LOW)
            log_here = log[0, head : head + 1, span]
            delta_here = delta[head : head + 1, span]
            acc = jnp.zeros((HD, TILE), F32)
            for j in range(i + 1):
                keys = slice(j * TILE, (j + 1) * TILE)
                part = lax.dot_general(k[keys, :], mine, NT, preferred_element_type=F32)
                probs = jnp.exp(part - log_here)
                if i == j:
                    probs = jnp.where(causal(part.shape), probs, 0.0)
                d_probs = lax.dot_general(v[keys, :], mine_do, NT, preferred_element_type=F32)
                d_scores = (probs * (d_probs - delta_here)).astype(LOW)
                dv[keys, :] += jnp.dot(probs.astype(LOW), mine_do, preferred_element_type=F32)
                dk[keys, :] += jnp.dot(d_scores, mine, preferred_element_type=F32)
                acc += jnp.dot(k_turn[rows, keys], d_scores, preferred_element_type=F32)
            dq_turn[rows, span] = acc * HD ** (-0.5)
    flat[...] = dq_turn[...].T
    for b in range(count):
        here = slice(b * block, (b + 1) * block)
        there = pl.ds(pl.multiple_of(order[b] * block, block), block)
        c, s = cos[there, :], sin[there, :]
        u = flat[there, :].astype(LOW).astype(F32)
        dq_out[here, :] = (u * c - half_turn(u) * s).astype(LOW)
        u = dk[there, :].astype(LOW).astype(F32)
        dk_out[here, :] = (u * c - half_turn(u) * s).astype(LOW)
        dv_out[here, :] = dv[there, :].astype(LOW)


def attend_backward(q, k, v, o, grad, log, order, cos, sin, block):
    length, group = q.shape
    pairs = group // PAIR
    whole = pl.BlockSpec((length, PAIR), lambda p, order: (0, p))
    table = pl.BlockSpec((length, PAIR), lambda p, order: (0, 0))
    low = jax.ShapeDtypeStruct((length, group), LOW)
    return pl.pallas_call(
        functools.partial(attend_back_kernel, block),
        grid_spec=pltpu.PrefetchScalarGridSpec(
            num_scalar_prefetch=1,
            grid=(pairs,),
            in_specs=[whole] * 5 + [pl.BlockSpec((1, 2, length), lambda p, order: (p, 0, 0)), table, table],
            out_specs=[whole] * 3,
            scratch_shapes=[
                pltpu.VMEM((length, PAIR), LOW),
                pltpu.VMEM((PAIR, length), LOW),
                pltpu.VMEM((2, length), F32),
                pltpu.VMEM((length, PAIR), F32),
                pltpu.VMEM((length, PAIR), F32),
                pltpu.VMEM((PAIR, length), F32),
                pltpu.VMEM((length, PAIR), F32),
            ],
        ),
        out_shape=[low] * 3,
        compiler_params=pltpu.CompilerParams(vmem_limit_bytes=50 << 20),
        name="attend_backward",
    )(order, q, k, v, o, grad, log, cos, sin)


def pieces_of(width, seq, fsdp):
    piece = width // (seq * fsdp)
    for i in range(seq):
        for j in range(fsdp):
            here, there = i * fsdp + j, j * seq + i
            yield slice(here * piece, (here + 1) * piece), slice(there * piece, (there + 1) * piece)


def norm_kernel(seq, fsdp, which, gains, tokens, *refs):
    if which:
        terms, (middle, normed, flat) = refs[:-3], refs[-3:]
        block = terms[0].shape[0]
        each = len(terms) // 2
        for half in range(2):
            rows = slice(half * block, (half + 1) * block)
            total = tokens[rows, :].astype(F32)
            for term in terms[half * each : (half + 1) * each]:
                total = total + term[...].astype(F32)
            middle[rows, :] = total
        values = middle[...]
    else:
        normed, flat = refs
        values = tokens[...].astype(F32)
    normal = values * rms_scale(values)
    for here, there in pieces_of(normal.shape[1], seq, fsdp):
        flat[:, there] = normal[:, here]
    normed[...] = (flat[...] * gains[which : which + 1, :].astype(F32)).astype(LOW)


def norm_back_kernel(seq, fsdp, which, gains, source, straight, *refs):
    count = len([r for r in refs if r.shape[0] * 2 == source.shape[0]])
    terms, outs, (flat, sums) = refs[:count], refs[count:-2], refs[-2:]
    block = terms[0].shape[0]
    each = count // 2
    for half in range(2):
        total = None
        for term in terms[half * each : (half + 1) * each]:
            total = term[...].astype(F32) if total is None else total + term[...].astype(F32)
        sums[half * block : (half + 1) * block, :] = total * gains[which : which + 1, :].astype(F32)
    for here, there in pieces_of(source.shape[1], seq, fsdp):
        flat[:, here] = sums[:, there]
    values = source[...].astype(F32)
    scale = rms_scale(values)
    normal = values * scale
    grad = flat[...]
    total = straight[...].astype(F32) + scale * (
        grad - normal * jnp.mean(grad * normal, axis=-1, keepdims=True)
    )
    for out in outs:
        out[...] = total.astype(out.dtype)


def norm_call(kernel, name, counts, which, gains, args, sums, outs, steps=1):
    size, width = args[0].shape
    rows = size // steps
    whole = pl.BlockSpec((rows, width), lambda i: (i, 0))
    half = pl.BlockSpec((rows // 2, width), lambda i: (0, 0))
    flat = pltpu.VMEM((rows, width), F32)
    return pl.pallas_call(
        functools.partial(kernel, counts["seq"], counts["fsdp"], which),
        grid=(steps,),
        in_specs=[pl.BlockSpec(gains.shape, lambda i: (0, 0))] + [whole] * len(args) + [half] * len(sums),
        out_specs=[whole] * len(outs),
        out_shape=[jax.ShapeDtypeStruct((size, width), dtype) for dtype in outs],
        scratch_shapes=[flat] if kernel is norm_kernel else [flat, flat],
        compiler_params=pltpu.CompilerParams(vmem_limit_bytes=40 << 20),
        name=name,
    )(gains, *args, *sums)


def flip(values, axis, count, mask):
    return lax.ppermute(values, axis, [(i, i ^ mask) for i in range(count)])


def bits_of(count):
    return list(range(count.bit_length() - 1))


def token_bits(count, half):
    bits = bits_of(count)
    return bits[:1] + (bits[1:] if half == 0 else bits[:0:-1])


def by_core(parts):
    middle = len(parts[0]) // 2
    return parts[0][:middle] + parts[1][:middle] + parts[0][middle:] + parts[1][middle:]


def token_order(count):
    me = lax.axis_index("seq")
    parts = []
    for half in (0, 1):
        ranks = [0]
        for bit in reversed(token_bits(count, half)):
            ranks = ranks + [rank ^ (1 << bit) for rank in ranks]
        parts.append([(me ^ rank) * 2 + half for rank in ranks])
    return jnp.stack(by_core(parts)).astype(jnp.int32)


def after(values, *others):
    return lax.optimization_barrier((values,) + others)[0]


def gather_tokens(values, count):
    rows = values.shape[0] // 2
    parts = []
    for half in (0, 1):
        part = [values[half * rows : (half + 1) * rows]]
        for bit in reversed(token_bits(count, half)):
            part = part + [flip(block, "seq", count, 1 << bit) for block in part]
        parts.append(part)
    return jnp.concatenate(by_core(parts), 0)


def reduce_tokens(values, weight, dims, count, pins=(), parts=1):
    size = values.shape[0] // 2

    def part(rows):
        return lax.dot_general(rows, weight, (dims, ((), ())), preferred_element_type=F32)

    def pinned(step, got, kept):
        return pins[step](got, kept) if step < len(pins) and pins[step] else got

    rows = size // parts
    got = [
        flip(part(values[size + i * rows : size + (i + 1) * rows]).astype(LOW), "seq", count, 1)
        for i in range(parts)
    ]
    kept = [part(values[i * rows : (i + 1) * rows]) for i in range(parts)]
    kept = [k + g.astype(F32) for k, g in zip(kept, pinned(0, got, kept))]
    if parts == 1:
        kept = [kept[0][: size // 2], kept[0][size // 2 :]]
    for step in range(1, count.bit_length() - 1):
        got = []
        for half in (0, 1):
            middle = kept[half].shape[0] // 2
            sent = kept[half][middle:].astype(LOW)
            kept[half] = kept[half][:middle]
            got.append(flip(sent, "seq", count, 1 << token_bits(count, half)[step]))
        got = pinned(step, got, kept)
        if step < count.bit_length() - 2:
            kept = [k + g.astype(F32) for k, g in zip(kept, got)]
    return [kept[0], got[0], kept[1], got[1]]


def per_device(
    counts, tokens, cotangent, attn_gain, mlp_gain, w_q, w_k, w_v, w_o, w_gate, w_up, w_down
):
    seq, fsdp = counts["seq"], counts["fsdp"]
    rows = tokens.shape[1]
    width = tokens.shape[2]
    block = rows // 2
    length = rows * seq
    own_tokens = tokens[0]
    own_grad = cotangent[0]
    group = HEADS // seq * HD
    hidden = w_gate.shape[1] // seq
    wrows = w_q.shape[0]
    def swap(*weights):
        piece = jnp.concatenate([w.reshape(wrows, seq, -1) for w in weights], -1)
        return lax.all_to_all(piece, "seq", split_axis=1, concat_axis=0, tiled=True).reshape(seq * wrows, -1)

    def swap_back(piece):
        return lax.all_to_all(
            piece.reshape(seq, wrows, -1), "seq", split_axis=0, concat_axis=1, tiled=False
        )

    def gathered(piece):
        return lax.all_gather(piece, "fsdp", axis=0, tiled=True)

    def summed(whole):
        return lax.psum_scatter(whole, "fsdp", scatter_dimension=0, tiled=True)

    def outer(left, right):
        return jnp.einsum("ti,to->io", left, right, preferred_element_type=F32).astype(LOW)

    near = jnp.zeros((wrows, LANES), LOW).at[:, 0].set(attn_gain).at[:, 1].set(mlp_gain)
    near = jnp.broadcast_to(near[:, None], (wrows, seq, LANES)).reshape(wrows, seq * LANES)
    qkv_piece = swap(w_q, w_k, w_v, near)
    pair_piece = swap(after(w_gate, qkv_piece), w_up)
    down_first = gathered(w_down[:, : width // 2])
    tall = seq * wrows
    wide = 4 * group
    piece = jnp.concatenate([qkv_piece[:, : 3 * group], w_o.reshape(tall, group)], -1)
    own_gains = qkv_piece[:, 3 * group : 3 * group + 2].T
    extra = GAIN_ROWS * -(-2 * tall // (GAIN_ROWS * wide))
    own_gains = jnp.pad(own_gains.reshape(-1), (0, extra * wide - 2 * tall)).reshape(extra, wide)
    first = gathered(after(jnp.concatenate([piece, own_gains], 0), down_first)).reshape(fsdp, tall + extra, wide)
    qkv_weight = first[:, :tall, : 3 * group].reshape(width, 3 * group)
    out_weight = first[:, :tall, 3 * group :].reshape(group, width)
    gains = first[:, tall:].reshape(fsdp, -1)[:, : 2 * tall].reshape(fsdp, 2, tall).swapaxes(0, 1).reshape(2, width)
    grad_out = gather_tokens(after(own_grad, pair_piece), seq)
    pair_weight = gathered(after(pair_piece, first, grad_out))
    down_last = gathered(after(w_down[:, width // 2 :], pair_weight))

    (normed_one,) = norm_call(
        norm_kernel, "norm_one", counts, 0, gains, [after(gather_tokens(own_tokens, seq), pair_piece)], [], [LOW], seq
    )
    order = token_order(seq)
    cosine, sine = rotary_tables(length)
    qkv = jnp.dot(normed_one, qkv_weight, preferred_element_type=F32)
    queries, keys, values, attended, logs = attend_forward(qkv, order, cosine, sine, block)
    sums = reduce_tokens(attended, out_weight, ((1,), (0,)), seq, parts=2)
    middle, own_two = norm_call(
        norm_kernel, "norm_two", counts, 1, gains, [own_tokens], sums, [F32, LOW]
    )
    normed_two = gather_tokens(own_two, seq)
    gates = jnp.dot(normed_two, pair_weight, preferred_element_type=F32)
    gate, up = gates[:, :hidden], gates[:, hidden:]
    sigmoid = jax.nn.sigmoid(gate)
    mixed = (gate * sigmoid * up).astype(LOW)
    down_whole = outer(mixed, grad_out)
    down_part = summed(after(down_whole, down_last))
    cot = after(grad_out, down_whole)
    grad_mixed = jnp.einsum(
        "td,fd->tf", cot[:, : width // 2], down_first, preferred_element_type=F32
    ) + jnp.einsum("td,fd->tf", cot[:, width // 2 :], down_last, preferred_element_type=F32)
    down_weight = jnp.concatenate([down_first, down_last], -1)
    grad_gate = (grad_mixed * up * sigmoid * (1.0 + gate * (1.0 - sigmoid))).astype(LOW)
    grad_up = (grad_mixed * gate * sigmoid).astype(LOW)
    grad_pair = jnp.concatenate([grad_gate, grad_up], -1)
    pair_whole = []

    def beside_pair(got, kept):
        pair_whole.append(outer(normed_two, after(grad_pair, *kept)))
        return got

    def after_pair(got, kept):
        return [after(g, pair_whole[0]) for g in got]

    sums = reduce_tokens(grad_pair, pair_weight, ((1,), (1,)), seq, [beside_pair, after_pair])
    pair_part = summed(after(pair_whole[0], down_part))
    grad_middle, own_proj = norm_call(
        norm_back_kernel, "norm_two_back", counts, 1, gains, [middle, own_grad], sums, [F32, LOW]
    )
    grad_proj = gather_tokens(own_proj, seq)

    out_whole = outer(attended, grad_proj)
    marks = []

    def hold(got, kept):
        marks.extend(kept)
        return [after(g, grad_proj) for g in got]

    def ahead(got, kept):
        marks.extend(got)
        return got

    down = reduce_tokens(after(mixed, own_proj), down_weight, ((1,), (0,)), seq, [hold, ahead])
    down_sum = jnp.concatenate([down[0] + down[1].astype(F32), down[2] + down[3].astype(F32)], 0)
    layer_out = (middle + down_sum).astype(LOW)[None]
    grad_heads = jnp.einsum(
        "to,io->ti", after(grad_proj, marks[0]), out_weight, preferred_element_type=F32
    ).astype(LOW)
    grad_qkv = jnp.concatenate(
        attend_backward(queries, keys, values, attended, grad_heads, logs, order, cosine, sine, block), -1
    )
    qkv_whole = outer(normed_one, after(grad_qkv, *marks[1:]))
    ready = []

    def early(got, kept):
        ready.extend(kept)
        return got

    sums = reduce_tokens(after(grad_qkv, qkv_whole), qkv_weight, ((1,), (1,)), seq, [early])
    (grad_inputs,) = norm_call(
        norm_back_kernel, "norm_one_back", counts, 0, gains, [own_tokens, grad_middle], sums, [LOW]
    )
    qkv_part = summed(after(qkv_whole, pair_part, *ready))
    out_part = summed(after(out_whole, qkv_part))

    def finish(piece, weight):
        piece = piece.reshape(wrows, -1).astype(F32)
        return piece, jnp.sum(piece * weight.astype(F32), axis=-1)

    pair_near = swap_back(pair_part)
    grad_gate_w, gate_gain = finish(pair_near[:, :, :hidden], w_gate)
    grad_up_w, up_gain = finish(pair_near[:, :, hidden:], w_up)
    qkv_near = swap_back(qkv_part)
    grad_q_w, q_gain = finish(qkv_near[:, :, :group], w_q)
    grad_k_w, k_gain = finish(qkv_near[:, :, group : 2 * group], w_k)
    grad_v_w, v_gain = finish(qkv_near[:, :, 2 * group :], w_v)
    return (
        layer_out,
        grad_inputs[None],
        (q_gain + k_gain + v_gain) / attn_gain.astype(F32),
        (gate_gain + up_gain) / mlp_gain.astype(F32),
        grad_q_w,
        grad_k_w,
        grad_v_w,
        out_part.astype(F32),
        grad_gate_w,
        grad_up_w,
        down_part.astype(F32),
    )


def solution(mesh):
    tokens = P("fsdp", "seq", None)
    vector = P(("seq", "fsdp"))
    matrix = P(("seq", "fsdp"), None)
    return jax.shard_map(
        functools.partial(per_device, dict(mesh.shape)),
        mesh=mesh,
        in_specs=(tokens, tokens, vector, vector) + (matrix,) * 7,
        out_specs=(tokens, tokens, vector, vector) + (matrix,) * 7,
        check_vma=False,
    )
```

```python
import functools

import jax
import jax.numpy as jnp
from jax import lax
from jax.experimental import pallas as pl
from jax.experimental.pallas import tpu as pltpu
from jax.sharding import PartitionSpec as P

HEADS = 32
HD = 64
PAIR = 2 * HD
LANES = 128
GAIN_ROWS = 16
TILE = 256
NT = (((1,), (1,)), ((), ()))

EPS = 1e-05
THETA = 130000.0

F32 = jnp.float32
LOW = jnp.bfloat16


def rms_scale(values):
    return lax.rsqrt(jnp.mean(values * values, axis=-1, keepdims=True) + EPS)


def rotary_tables(length):
    halfway = HD // 2
    frequency = THETA ** (-(jnp.arange(halfway, dtype=F32) * 2.0) / HD)
    angles = jnp.arange(length, dtype=jnp.int32).astype(F32)[:, None] * frequency[None, :]
    cosine = jnp.cos(angles)
    sine = jnp.sin(angles)
    return (
        jnp.concatenate([cosine, cosine, cosine, cosine], -1),
        jnp.concatenate([-sine, sine, -sine, sine], -1),
    )


def head_lanes(head):
    lane = lax.broadcasted_iota(jnp.int32, (1, PAIR), 1)
    return (lane >= head * HD) & (lane < (head + 1) * HD)


def half_turn(values):
    lane = lax.broadcasted_iota(jnp.int32, values.shape, 1)
    return jnp.where(
        lane % HD < HD // 2,
        pltpu.roll(values, PAIR - HD // 2, 1),
        pltpu.roll(values, HD // 2, 1),
    )


def causal(shape):
    return lax.broadcasted_iota(jnp.int32, shape, 0) <= lax.broadcasted_iota(jnp.int32, shape, 1)


def attend_kernel(
    block, order, q, k, v, cos, sin, q_out, k_out, v_out, o_out, log_out,
    v_turn, o_turn, o_flat, scores,
):
    length = q_out.shape[0]
    count = length // block
    for b in range(count):
        here = slice(b * block, (b + 1) * block)
        there = pl.ds(pl.multiple_of(order[b] * block, block), block)
        c, s = cos[there, :], sin[there, :]
        u = q[here, :]
        q_out[there, :] = (u * c + half_turn(u) * s).astype(LOW)
        u = k[here, :]
        k_out[there, :] = (u * c + half_turn(u) * s).astype(LOW)
        v_out[there, :] = v[here, :].astype(LOW)
    v_turn[...] = v_out[...].astype(F32).T.astype(LOW)
    for i in range(length // TILE):
        queries = q_out[i * TILE : (i + 1) * TILE, :] * HD ** (-0.5)
        for head in range(2):
            mine = jnp.where(head_lanes(head), queries, 0).astype(LOW)
            rows = slice(head * HD, (head + 1) * HD)
            highest = None
            for j in range(i + 1):
                part = lax.dot_general(
                    k_out[j * TILE : (j + 1) * TILE, :], mine, NT, preferred_element_type=F32
                )
                if i == j:
                    part = jnp.where(causal(part.shape), part, -1e30)
                scores[head, j * TILE : (j + 1) * TILE, :] = part
                top = jnp.max(part, axis=0, keepdims=True)
                highest = top if highest is None else jnp.maximum(highest, top)
            total = jnp.zeros((1, TILE), F32)
            acc = jnp.zeros((HD, TILE), F32)
            for j in range(i + 1):
                weights = jnp.exp(scores[head, j * TILE : (j + 1) * TILE, :] - highest)
                total += jnp.sum(weights, axis=0, keepdims=True)
                acc += jnp.dot(
                    v_turn[rows, j * TILE : (j + 1) * TILE], weights.astype(LOW), preferred_element_type=F32
                )
            o_turn[rows, i * TILE : (i + 1) * TILE] = acc / total
            log_out[0, head : head + 1, i * TILE : (i + 1) * TILE] = highest + jnp.log(total)
    o_flat[...] = o_turn[...].T
    for b in range(count):
        there = pl.ds(pl.multiple_of(order[b] * block, block), block)
        o_out[b * block : (b + 1) * block, :] = o_flat[there, :].astype(LOW)


def attend_forward(qkv, order, cos, sin, block):
    length, group = qkv.shape[0], qkv.shape[1] // 3
    pairs = group // PAIR

    def column(which):
        return pl.BlockSpec((length, PAIR), lambda p, order: (0, which * pairs + p))

    whole = pl.BlockSpec((length, PAIR), lambda p, order: (0, p))
    table = pl.BlockSpec((length, PAIR), lambda p, order: (0, 0))
    low = jax.ShapeDtypeStruct((length, group), LOW)
    return pl.pallas_call(
        functools.partial(attend_kernel, block),
        grid_spec=pltpu.PrefetchScalarGridSpec(
            num_scalar_prefetch=1,
            grid=(pairs,),
            in_specs=[column(0), column(1), column(2), table, table],
            out_specs=[whole] * 4 + [pl.BlockSpec((1, 2, length), lambda p, order: (p, 0, 0))],
            scratch_shapes=[
                pltpu.VMEM((PAIR, length), LOW),
                pltpu.VMEM((PAIR, length), F32),
                pltpu.VMEM((length, PAIR), F32),
                pltpu.VMEM((2, length, TILE), F32),
            ],
        ),
        out_shape=[low] * 4 + [jax.ShapeDtypeStruct((pairs, 2, length), F32)],
        compiler_params=pltpu.CompilerParams(vmem_limit_bytes=50 << 20),
        name="attend_forward",
    )(order, qkv, qkv, qkv, cos, sin)


def attend_back_kernel(
    block, order, q, k, v, o, grad, log, cos, sin, dq_out, dk_out, dv_out,
    do, k_turn, delta, dk, dv, dq_turn, flat,
):
    length = q.shape[0]
    count = length // block
    for b in range(count):
        here = slice(b * block, (b + 1) * block)
        there = pl.ds(pl.multiple_of(order[b] * block, block), block)
        do[there, :] = grad[here, :]
        flat[there, :] = grad[here, :].astype(F32) * o[here, :].astype(F32)
    turned = flat[...].T
    for head in range(2):
        delta[head : head + 1, :] = jnp.sum(turned[head * HD : (head + 1) * HD], axis=0, keepdims=True)
    k_turn[...] = k[...].astype(F32).T.astype(LOW)
    dk[...] = jnp.zeros_like(dk)
    dv[...] = jnp.zeros_like(dv)
    for i in range(length // TILE):
        span = slice(i * TILE, (i + 1) * TILE)
        queries = q[span, :] * HD ** (-0.5)
        for head in range(2):
            lanes = head_lanes(head)
            rows = slice(head * HD, (head + 1) * HD)
            mine = jnp.where(lanes, queries, 0).astype(LOW)
            mine_do = jnp.where(lanes, do[span, :], 0).astype(LOW)
            log_here = log[0, head : head + 1, span]
            delta_here = delta[head : head + 1, span]
            acc = jnp.zeros((HD, TILE), F32)
            for j in range(i + 1):
                keys = slice(j * TILE, (j + 1) * TILE)
                part = lax.dot_general(k[keys, :], mine, NT, preferred_element_type=F32)
                probs = jnp.exp(part - log_here)
                if i == j:
                    probs = jnp.where(causal(part.shape), probs, 0.0)
                d_probs = lax.dot_general(v[keys, :], mine_do, NT, preferred_element_type=F32)
                d_scores = (probs * (d_probs - delta_here)).astype(LOW)
                dv[keys, :] += jnp.dot(probs.astype(LOW), mine_do, preferred_element_type=F32)
                dk[keys, :] += jnp.dot(d_scores, mine, preferred_element_type=F32)
                acc += jnp.dot(k_turn[rows, keys], d_scores, preferred_element_type=F32)
            dq_turn[rows, span] = acc * HD ** (-0.5)
    flat[...] = dq_turn[...].T
    for b in range(count):
        here = slice(b * block, (b + 1) * block)
        there = pl.ds(pl.multiple_of(order[b] * block, block), block)
        c, s = cos[there, :], sin[there, :]
        u = flat[there, :].astype(LOW).astype(F32)
        dq_out[here, :] = (u * c - half_turn(u) * s).astype(LOW)
        u = dk[there, :].astype(LOW).astype(F32)
        dk_out[here, :] = (u * c - half_turn(u) * s).astype(LOW)
        dv_out[here, :] = dv[there, :].astype(LOW)


def attend_backward(q, k, v, o, grad, log, order, cos, sin, block):
    length, group = q.shape
    pairs = group // PAIR
    whole = pl.BlockSpec((length, PAIR), lambda p, order: (0, p))
    table = pl.BlockSpec((length, PAIR), lambda p, order: (0, 0))
    low = jax.ShapeDtypeStruct((length, group), LOW)
    return pl.pallas_call(
        functools.partial(attend_back_kernel, block),
        grid_spec=pltpu.PrefetchScalarGridSpec(
            num_scalar_prefetch=1,
            grid=(pairs,),
            in_specs=[whole] * 5 + [pl.BlockSpec((1, 2, length), lambda p, order: (p, 0, 0)), table, table],
            out_specs=[whole] * 3,
            scratch_shapes=[
                pltpu.VMEM((length, PAIR), LOW),
                pltpu.VMEM((PAIR, length), LOW),
                pltpu.VMEM((2, length), F32),
                pltpu.VMEM((length, PAIR), F32),
                pltpu.VMEM((length, PAIR), F32),
                pltpu.VMEM((PAIR, length), F32),
                pltpu.VMEM((length, PAIR), F32),
            ],
        ),
        out_shape=[low] * 3,
        compiler_params=pltpu.CompilerParams(vmem_limit_bytes=50 << 20),
        name="attend_backward",
    )(order, q, k, v, o, grad, log, cos, sin)


def pieces_of(width, seq, fsdp):
    piece = width // (seq * fsdp)
    for i in range(seq):
        for j in range(fsdp):
            here, there = i * fsdp + j, j * seq + i
            yield slice(here * piece, (here + 1) * piece), slice(there * piece, (there + 1) * piece)


def norm_kernel(seq, fsdp, which, gains, tokens, *refs):
    if which:
        terms, (middle, normed, flat) = refs[:-3], refs[-3:]
        block = terms[0].shape[0]
        each = len(terms) // 2
        for half in range(2):
            rows = slice(half * block, (half + 1) * block)
            total = tokens[rows, :].astype(F32)
            for term in terms[half * each : (half + 1) * each]:
                total = total + term[...].astype(F32)
            middle[rows, :] = total
        values = middle[...]
    else:
        normed, flat = refs
        values = tokens[...].astype(F32)
    normal = values * rms_scale(values)
    for here, there in pieces_of(normal.shape[1], seq, fsdp):
        flat[:, there] = normal[:, here]
    normed[...] = (flat[...] * gains[which : which + 1, :].astype(F32)).astype(LOW)


def norm_back_kernel(seq, fsdp, which, gains, source, straight, *refs):
    count = len([r for r in refs if r.shape[0] * 2 == source.shape[0]])
    terms, outs, (flat, sums) = refs[:count], refs[count:-2], refs[-2:]
    block = terms[0].shape[0]
    each = count // 2
    for half in range(2):
        total = None
        for term in terms[half * each : (half + 1) * each]:
            total = term[...].astype(F32) if total is None else total + term[...].astype(F32)
        sums[half * block : (half + 1) * block, :] = total * gains[which : which + 1, :].astype(F32)
    for here, there in pieces_of(source.shape[1], seq, fsdp):
        flat[:, here] = sums[:, there]
    values = source[...].astype(F32)
    scale = rms_scale(values)
    normal = values * scale
    grad = flat[...]
    total = straight[...].astype(F32) + scale * (
        grad - normal * jnp.mean(grad * normal, axis=-1, keepdims=True)
    )
    for out in outs:
        out[...] = total.astype(out.dtype)


def norm_call(kernel, name, counts, which, gains, args, sums, outs, steps=1):
    size, width = args[0].shape
    rows = size // steps
    whole = pl.BlockSpec((rows, width), lambda i: (i, 0))
    half = pl.BlockSpec((rows // 2, width), lambda i: (0, 0))
    flat = pltpu.VMEM((rows, width), F32)
    return pl.pallas_call(
        functools.partial(kernel, counts["seq"], counts["fsdp"], which),
        grid=(steps,),
        in_specs=[pl.BlockSpec(gains.shape, lambda i: (0, 0))] + [whole] * len(args) + [half] * len(sums),
        out_specs=[whole] * len(outs),
        out_shape=[jax.ShapeDtypeStruct((size, width), dtype) for dtype in outs],
        scratch_shapes=[flat] if kernel is norm_kernel else [flat, flat],
        compiler_params=pltpu.CompilerParams(vmem_limit_bytes=40 << 20),
        name=name,
    )(gains, *args, *sums)


def flip(values, axis, count, mask):
    return lax.ppermute(values, axis, [(i, i ^ mask) for i in range(count)])


def bits_of(count):
    return list(range(count.bit_length() - 1))


def token_bits(count, half):
    bits = bits_of(count)
    return bits[:1] + (bits[1:] if half == 0 else bits[:0:-1])


def by_core(parts):
    middle = len(parts[0]) // 2
    return parts[0][:middle] + parts[1][:middle] + parts[0][middle:] + parts[1][middle:]


def token_order(count):
    me = lax.axis_index("seq")
    parts = []
    for half in (0, 1):
        ranks = [0]
        for bit in reversed(token_bits(count, half)):
            ranks = ranks + [rank ^ (1 << bit) for rank in ranks]
        parts.append([(me ^ rank) * 2 + half for rank in ranks])
    return jnp.stack(by_core(parts)).astype(jnp.int32)


def after(values, *others):
    return lax.optimization_barrier((values,) + others)[0]


def gather_tokens(values, count):
    rows = values.shape[0] // 2
    parts = []
    for half in (0, 1):
        part = [values[half * rows : (half + 1) * rows]]
        for bit in reversed(token_bits(count, half)):
            part = part + [flip(block, "seq", count, 1 << bit) for block in part]
        parts.append(part)
    return jnp.concatenate(by_core(parts), 0)


def reduce_tokens(values, weight, dims, count, pins=(), parts=1):
    size = values.shape[0] // 2

    def part(rows):
        return lax.dot_general(rows, weight, (dims, ((), ())), preferred_element_type=F32)

    def pinned(step, got, kept):
        return pins[step](got, kept) if step < len(pins) and pins[step] else got

    rows = size // parts
    got = [
        flip(part(values[size + i * rows : size + (i + 1) * rows]).astype(LOW), "seq", count, 1)
        for i in range(parts)
    ]
    kept = [part(values[i * rows : (i + 1) * rows]) for i in range(parts)]
    kept = [k + g.astype(F32) for k, g in zip(kept, pinned(0, got, kept))]
    if parts == 1:
        kept = [kept[0][: size // 2], kept[0][size // 2 :]]
    for step in range(1, count.bit_length() - 1):
        got = []
        for half in (0, 1):
            middle = kept[half].shape[0] // 2
            sent = kept[half][middle:].astype(LOW)
            kept[half] = kept[half][:middle]
            got.append(flip(sent, "seq", count, 1 << token_bits(count, half)[step]))
        got = pinned(step, got, kept)
        if step < count.bit_length() - 2:
            kept = [k + g.astype(F32) for k, g in zip(kept, got)]
    return [kept[0], got[0], kept[1], got[1]]


def per_device(
    counts, tokens, cotangent, attn_gain, mlp_gain, w_q, w_k, w_v, w_o, w_gate, w_up, w_down
):
    seq, fsdp = counts["seq"], counts["fsdp"]
    rows = tokens.shape[1]
    width = tokens.shape[2]
    block = rows // 2
    length = rows * seq
    own_tokens = tokens[0]
    own_grad = cotangent[0]
    group = HEADS // seq * HD
    hidden = w_gate.shape[1] // seq
    wrows = w_q.shape[0]
    def swap(*weights):
        piece = jnp.concatenate([w.reshape(wrows, seq, -1) for w in weights], -1)
        return lax.all_to_all(piece, "seq", split_axis=1, concat_axis=0, tiled=True).reshape(seq * wrows, -1)

    def swap_back(piece):
        return lax.all_to_all(
            piece.reshape(seq, wrows, -1), "seq", split_axis=0, concat_axis=1, tiled=False
        )

    def gathered(piece):
        return lax.all_gather(piece, "fsdp", axis=0, tiled=True)

    def summed(whole):
        return lax.psum_scatter(whole, "fsdp", scatter_dimension=0, tiled=True)

    def outer(left, right):
        return jnp.einsum("ti,to->io", left, right, preferred_element_type=F32).astype(LOW)

    near = jnp.zeros((wrows, LANES), LOW).at[:, 0].set(attn_gain).at[:, 1].set(mlp_gain)
    near = jnp.broadcast_to(near[:, None], (wrows, seq, LANES)).reshape(wrows, seq * LANES)
    qkv_piece = swap(w_q, w_k, w_v, near)
    pair_piece = swap(after(w_gate, qkv_piece), w_up)
    cut = width * 3 // 8
    down_first = gathered(w_down[:, :cut])
    tall = seq * wrows
    wide = 4 * group
    piece = jnp.concatenate([qkv_piece[:, : 3 * group], w_o.reshape(tall, group)], -1)
    own_gains = qkv_piece[:, 3 * group : 3 * group + 2].T
    extra = GAIN_ROWS * -(-2 * tall // (GAIN_ROWS * wide))
    own_gains = jnp.pad(own_gains.reshape(-1), (0, extra * wide - 2 * tall)).reshape(extra, wide)
    first = gathered(after(jnp.concatenate([piece, own_gains], 0), down_first)).reshape(fsdp, tall + extra, wide)
    qkv_weight = first[:, :tall, : 3 * group].reshape(width, 3 * group)
    out_weight = first[:, :tall, 3 * group :].reshape(group, width)
    gains = first[:, tall:].reshape(fsdp, -1)[:, : 2 * tall].reshape(fsdp, 2, tall).swapaxes(0, 1).reshape(2, width)
    grad_out = gather_tokens(after(own_grad, pair_piece), seq)
    pair_weight = gathered(after(pair_piece, first, grad_out))
    down_last = gathered(after(w_down[:, cut:], pair_weight))

    (normed_one,) = norm_call(
        norm_kernel, "norm_one", counts, 0, gains, [after(gather_tokens(own_tokens, seq), pair_piece)], [], [LOW], seq
    )
    order = token_order(seq)
    cosine, sine = rotary_tables(length)
    qkv = jnp.dot(normed_one, qkv_weight, preferred_element_type=F32)
    queries, keys, values, attended, logs = attend_forward(qkv, order, cosine, sine, block)
    sums = reduce_tokens(attended, out_weight, ((1,), (0,)), seq, parts=2)
    middle, own_two = norm_call(
        norm_kernel, "norm_two", counts, 1, gains, [own_tokens], sums, [F32, LOW]
    )
    normed_two = gather_tokens(own_two, seq)
    gates = jnp.dot(normed_two, pair_weight, preferred_element_type=F32)
    gate, up = gates[:, :hidden], gates[:, hidden:]
    sigmoid = jax.nn.sigmoid(gate)
    mixed = (gate * sigmoid * up).astype(LOW)
    down_whole = outer(mixed, grad_out)
    down_part = summed(after(down_whole, down_last))
    cot = after(grad_out, down_whole)
    grad_mixed = jnp.einsum(
        "td,fd->tf", cot[:, :cut], down_first, preferred_element_type=F32
    ) + jnp.einsum("td,fd->tf", cot[:, cut:], down_last, preferred_element_type=F32)
    down_weight = jnp.concatenate([down_first, down_last], -1)
    grad_gate = (grad_mixed * up * sigmoid * (1.0 + gate * (1.0 - sigmoid))).astype(LOW)
    grad_up = (grad_mixed * gate * sigmoid).astype(LOW)
    grad_pair = jnp.concatenate([grad_gate, grad_up], -1)
    pair_whole = []

    def beside_pair(got, kept):
        pair_whole.append(outer(normed_two, after(grad_pair, *kept)))
        return got

    def after_pair(got, kept):
        return [after(g, pair_whole[0]) for g in got]

    sums = reduce_tokens(grad_pair, pair_weight, ((1,), (1,)), seq, [beside_pair, after_pair])
    pair_part = summed(after(pair_whole[0], down_part))
    grad_middle, own_proj = norm_call(
        norm_back_kernel, "norm_two_back", counts, 1, gains, [middle, own_grad], sums, [F32, LOW]
    )
    grad_proj = gather_tokens(own_proj, seq)

    out_whole = outer(attended, grad_proj)
    marks = []

    def hold(got, kept):
        marks.extend(kept)
        return [after(g, grad_proj) for g in got]

    def ahead(got, kept):
        marks.extend(got)
        return got

    down = reduce_tokens(after(mixed, own_proj), down_weight, ((1,), (0,)), seq, [hold, ahead])
    down_sum = jnp.concatenate([down[0] + down[1].astype(F32), down[2] + down[3].astype(F32)], 0)
    layer_out = (middle + down_sum).astype(LOW)[None]
    grad_heads = jnp.einsum(
        "to,io->ti", after(grad_proj, marks[0]), out_weight, preferred_element_type=F32
    ).astype(LOW)
    grad_qkv = jnp.concatenate(
        attend_backward(queries, keys, values, attended, grad_heads, logs, order, cosine, sine, block), -1
    )
    qkv_whole = outer(normed_one, after(grad_qkv, *marks[1:]))
    ready = []

    def early(got, kept):
        ready.extend(kept)
        return got

    sums = reduce_tokens(after(grad_qkv, qkv_whole), qkv_weight, ((1,), (1,)), seq, [early])
    (grad_inputs,) = norm_call(
        norm_back_kernel, "norm_one_back", counts, 0, gains, [own_tokens, grad_middle], sums, [LOW]
    )
    qkv_part = summed(after(qkv_whole, pair_part, *ready))
    out_part = summed(after(out_whole, qkv_part))

    def finish(piece, weight):
        piece = piece.reshape(wrows, -1).astype(F32)
        return piece, jnp.sum(piece * weight.astype(F32), axis=-1)

    pair_near = swap_back(pair_part)
    grad_gate_w, gate_gain = finish(pair_near[:, :, :hidden], w_gate)
    grad_up_w, up_gain = finish(pair_near[:, :, hidden:], w_up)
    qkv_near = swap_back(qkv_part)
    grad_q_w, q_gain = finish(qkv_near[:, :, :group], w_q)
    grad_k_w, k_gain = finish(qkv_near[:, :, group : 2 * group], w_k)
    grad_v_w, v_gain = finish(qkv_near[:, :, 2 * group :], w_v)
    return (
        layer_out,
        grad_inputs[None],
        (q_gain + k_gain + v_gain) / attn_gain.astype(F32),
        (gate_gain + up_gain) / mlp_gain.astype(F32),
        grad_q_w,
        grad_k_w,
        grad_v_w,
        out_part.astype(F32),
        grad_gate_w,
        grad_up_w,
        down_part.astype(F32),
    )


def solution(mesh):
    tokens = P("fsdp", "seq", None)
    vector = P(("seq", "fsdp"))
    matrix = P(("seq", "fsdp"), None)
    return jax.shard_map(
        functools.partial(per_device, dict(mesh.shape)),
        mesh=mesh,
        in_specs=(tokens, tokens, vector, vector) + (matrix,) * 7,
        out_specs=(tokens, tokens, vector, vector) + (matrix,) * 7,
        check_vma=False,
    )
```
